32 devices in a mesh: dp: 4 (over z), section: 4 (over y, x), mp: 2 (over core).
Axes of the slice: x: 2, y: 2, z: 4, core: 2. Of those that a mesh axis runs over, the one named last changes fastest.
Arguments:
- inputs: bfloat16 [4, 128, 3072], P(None, 'dp'), may hold values from -6 to 6
- target: bfloat16 [4, 128, 3072], P(None, 'dp', 'mp'), may hold values from -6 to 6
- gains: float32 [4, 3072], P('section'), may hold values from 0.5 to 1.5
- weights: bfloat16 [4, 3072, 3072], P('section', 'dp', 'mp'), may hold values from -0.109375 to 0.109375
- probes: float32 [4, 4, 3072], P(None, 'section', 'dp'), may hold values from -6 to 6
Outputs:
- hvp: float32 [4, 4, 3072], P(None, 'section', 'dp')
- probes_next: float32 [4, 4, 3072], P(None, 'section', 'dp')
The draws below stay inside these ranges and needn't reach their ends.
All inputs are finite; a program needn't handle non-finite values.
Results may differ from the reference program's by a relative error of at most 0.013.
Values may be sent and summed in bfloat16 or wider, within the bound.
A program may use at most 128 MiB of HBM per device.

```python
import math
import jax
import jax.numpy as jnp
from jax import lax

D = 3072
PROBES = 4
MB = 4
TOKENS = 128
SECTIONS = 4


def steps_of(key, dims, shards, least, largest):
    level = 1.0
    for dim, parts in shards:
        heights = jax.random.uniform(jax.random.fold_in(jax.random.fold_in(key, 6), dim), (parts,), jnp.float32, least / len(shards), largest / len(shards))
        level = level * jnp.repeat(jnp.exp(heights), dims[dim] // parts).reshape((-1,) + (1,) * (len(dims) - 1 - dim))
    return level


def gaussian(own_key, dims, width, bound, pieces=(), held_as=jnp.bfloat16):
    level = steps_of(own_key, dims, pieces, -0.22, 0.18) if pieces else 1.0
    entries = jax.random.normal(own_key, dims, jnp.float32) * width * level
    return jnp.minimum(jnp.maximum(entries, -bound), bound).astype(held_as)


def setup_inputs(seed: int = 0) -> dict:
    seeds = jax.random.split(jax.random.key(seed), 6)
    return {
        "inputs": gaussian(seeds[0], (MB, TOKENS, D), 1.0, 6.0, ((1, 4),)),
        "target": gaussian(seeds[1], (MB, TOKENS, D), 1.0, 6.0, ((1, 4), (2, 2))),
        "gains": jnp.clip(1.0 + 0.1 * jax.random.normal(seeds[2], (SECTIONS, D), jnp.float32), 0.5, 1.5),
        "weights": gaussian(seeds[3], (SECTIONS, D, D), D ** -0.5, 0.109375, ((0, 4), (1, 4), (2, 2))),
        "probes": gaussian(seeds[4], (PROBES, SECTIONS, D), 1.0, 6.0, ((1, 4), (2, 4)), jnp.float32),
    }


EPS = 1e-05
ETA = 0.5

def norm_parts(whole_input):
    values = whole_input.astype(jnp.float32)
    hidden = values[0]
    tangent = values[1:]
    scale_inv = lax.rsqrt(lax.optimization_barrier(jnp.mean(hidden * hidden, axis=-1, keepdims=True)) + EPS)
    normed = hidden * scale_inv
    scale_dot = -scale_inv ** 3 * lax.optimization_barrier(jnp.mean(hidden * tangent, axis=-1, keepdims=True))
    normed_dot = tangent * scale_inv + hidden * scale_dot
    return (hidden, tangent, scale_inv, normed, scale_dot, normed_dot)

def section_forward(whole_input, own_cols, gain_row, probe_dirs, weight):
    hidden, tangent, scale_inv, normed, scale_dot, normed_dot = norm_parts(whole_input)
    mixed_in = normed * gain_row
    mixed_dot = normed_dot * gain_row + normed[None] * probe_dirs[:, None, :]
    operand = jnp.concatenate([mixed_in[None], mixed_dot], axis=0).astype(jnp.bfloat16)
    flattened = operand.reshape(-1, operand.shape[-1])
    product = jnp.dot(flattened.astype(jnp.float32), weight.astype(jnp.float32), preferred_element_type=jnp.float32)
    product = product.reshape(operand.shape[:2] + (weight.shape[1],))
    active = jnp.tanh(product[0])
    active_dot = (1.0 - active * active) * product[1:]
    section_activity = jnp.concatenate([active[None], active_dot], axis=0)
    residual = own_cols.astype(jnp.float32)
    return ((residual + section_activity).astype(jnp.bfloat16), section_activity)

def section_backward(whole_input, gain_row, probe_dirs, weight, section_activity, cotangent):
    hidden, tangent, scale_inv, normed, scale_dot, normed_dot = norm_parts(whole_input)
    incoming = cotangent.astype(jnp.float32)
    active = section_activity[0]
    active_dot = section_activity[1:]
    derivative = 1.0 - active * active
    pre_grad = incoming[0] * derivative
    pre_dot = incoming[1:] * derivative - 2.0 * active * active_dot * incoming[0]
    operand = jnp.concatenate([pre_grad[None], pre_dot], axis=0).astype(jnp.bfloat16)
    flattened = operand.reshape(-1, operand.shape[-1])
    returned = jnp.dot(flattened.astype(jnp.float32), weight.T.astype(jnp.float32), preferred_element_type=jnp.float32)
    returned = returned.reshape(operand.shape[:2] + (weight.shape[0],))
    mixed_grad = returned[0]
    mixed_dot = returned[1:]
    gain_dot = lax.optimization_barrier(jnp.sum(mixed_dot * normed + mixed_grad * normed_dot, axis=1))
    normed_grad = mixed_grad * gain_row
    normed_gdot = mixed_dot * gain_row + mixed_grad * probe_dirs[:, None, :]
    features = hidden.shape[-1]
    inner_grad = lax.optimization_barrier(jnp.sum(normed_grad * hidden, axis=-1, keepdims=True))
    inner_dot = lax.optimization_barrier(jnp.sum(normed_gdot * hidden + normed_grad * tangent, axis=-1, keepdims=True))
    cube_scale = scale_inv ** 3 / features
    grad_in = scale_inv * normed_grad - cube_scale * hidden * inner_grad
    grad_dot = scale_dot * normed_grad + scale_inv * normed_gdot - 3.0 * scale_inv * scale_inv * scale_dot / features * hidden * inner_grad - cube_scale * tangent * inner_grad - cube_scale * hidden * inner_dot
    return (jnp.concatenate([grad_in[None], grad_dot], axis=0), gain_dot)

def reference(inputs, target, gains, weights, probes):
    curvature = [jnp.zeros((PROBES, D), jnp.float32) for section_id in range(SECTIONS)]
    blank = jnp.zeros((PROBES, TOKENS, D), jnp.bfloat16)
    for batch_id in range(MB):
        current = jnp.concatenate([inputs[batch_id][None], blank], axis=0)
        kept = []
        for section_id in range(SECTIONS):
            section_result, section_activity = section_forward(current, current, gains[section_id], probes[:, section_id, :], weights[section_id])
            kept.append((current, section_activity))
            current = section_result
        error = (current[0].astype(jnp.float32) - target[batch_id].astype(jnp.float32)).astype(jnp.bfloat16)
        cotangent = jnp.concatenate([error[None], current[1:]], axis=0)
        for section_id in reversed(range(SECTIONS)):
            whole_input, section_activity = kept[section_id]
            grads, gain_dot = section_backward(whole_input, gains[section_id], probes[:, section_id, :], weights[section_id], section_activity, cotangent)
            curvature[section_id] = curvature[section_id] + gain_dot
            cotangent = (grads + cotangent.astype(jnp.float32)).astype(jnp.bfloat16)
    hvp = jnp.stack(curvature, axis=1) / (MB * TOKENS)
    moved = probes + ETA * hvp
    matrix = moved.reshape(PROBES, SECTIONS * D)
    gram = jnp.dot(matrix, matrix.T, precision=lax.Precision.HIGHEST)
    factor = jnp.linalg.cholesky(gram)
    rotated = jax.scipy.linalg.solve_triangular(factor, matrix, lower=True) * math.sqrt(SECTIONS * D)
    return (hvp, rotated.reshape(PROBES, SECTIONS, D))
```

```python
import functools
import math

import jax
import jax.numpy as jnp
from jax import lax
from jax.experimental import pallas as pl
from jax.experimental.pallas import tpu as pltpu
from jax.sharding import PartitionSpec as P

EPS = 1e-05
ETA = 0.5
MESH = pl.DeviceIdType.MESH
F32 = jnp.float32
BF16 = jnp.bfloat16


def fold(values):
    total = values[..., 0:128]
    for start in range(128, values.shape[-1], 128):
        total = total + values[..., start : start + 128]
    return total


def relay_kernel(
    sections,
    lag_step,
    inputs_ref,
    target_ref,
    gain_ref,
    probe_ref,
    weight_ref,
    acc_ref,
    whole,
    act,
    out,
    cot_in,
    cot_out,
    part_out,
    part_in,
    operand,
    gstack,
    q,
    stats,
    hop_send,
    hop_recv,
    sib_send,
    sib_recv,
    part_send,
    part_recv,
    back_send,
    back_recv,
):
    pos = lax.axis_index("section")
    core = lax.axis_index("mp")
    last = sections - 1
    chunks, tokens, features = inputs_ref.shape
    cols = features // 2
    dirs = probe_ref.shape[1]
    tile = 512 if cols % 512 == 0 else 256 if cols % 256 == 0 else 128
    tiles = cols // tile

    barrier = pltpu.get_barrier_semaphore()
    pl.semaphore_signal(barrier, inc=1, device_id={"mp": 1 - core}, device_id_type=MESH)

    @pl.when(pos > 0)
    def _():
        pl.semaphore_signal(barrier, inc=1, device_id={"section": pos - 1}, device_id_type=MESH)

    @pl.when(pos < last)
    def _():
        pl.semaphore_signal(barrier, inc=1, device_id={"section": pos + 1}, device_id_type=MESH)

    peers = 1 + (pos > 0).astype(jnp.int32) + (pos < last).astype(jnp.int32)
    pl.semaphore_wait(barrier, peers)

    def hop(c):
        return pltpu.make_async_remote_copy(
            src_ref=out.at[c],
            dst_ref=whole.at[c, core],
            send_sem=hop_send.at[c],
            recv_sem=hop_recv.at[c],
            device_id={"section": pos + 1},
            device_id_type=MESH,
        )

    def sibling(c):
        return pltpu.make_async_remote_copy(
            src_ref=whole.at[c, core],
            dst_ref=whole.at[c, core],
            send_sem=sib_send.at[c],
            recv_sem=sib_recv.at[c],
            device_id={"mp": 1 - core},
            device_id_type=MESH,
        )

    def part(c):
        return pltpu.make_async_remote_copy(
            src_ref=part_out.at[c],
            dst_ref=part_in.at[c],
            send_sem=part_send.at[c],
            recv_sem=part_recv.at[c],
            device_id={"mp": 1 - core},
            device_id_type=MESH,
        )

    def back(c):
        return pltpu.make_async_remote_copy(
            src_ref=cot_out.at[c],
            dst_ref=cot_in.at[c],
            send_sem=back_send.at[c],
            recv_sem=back_recv.at[c],
            device_id={"section": pos - 1},
            device_id_type=MESH,
        )

    def rows(k):
        return pl.ds(k * tokens, tokens)

    acc_ref[...] = jnp.zeros_like(acc_ref)

    def forward(c):
        @pl.when(pos == 0)
        def _():
            for half in range(2):
                whole[c, half, 0:tokens, :] = inputs_ref[c, :, half * cols : (half + 1) * cols]
                whole[c, half, tokens:, :] = jnp.zeros((dirs * tokens, cols), BF16)

        @pl.when(pos > 0)
        def _():
            hop(c).wait_recv()
            swap = sibling(c)
            swap.start()
            swap.wait_recv()

        square = jnp.zeros((tokens, 128), F32)
        cross = [jnp.zeros((tokens, 128), F32) for _ in range(dirs)]
        for half in range(2):
            for j in range(tiles):
                at = pl.ds(j * tile, tile)
                h = whole[c, half, rows(0), at].astype(F32)
                square = square + fold(h * h)
                for k in range(dirs):
                    cross[k] = cross[k] + fold(h * whole[c, half, rows(k + 1), at].astype(F32))
        s = lax.rsqrt(jnp.sum(square, axis=-1, keepdims=True) / features + EPS)
        cube = -(s * s * s) / features
        u = [cube * jnp.sum(cross[k], axis=-1, keepdims=True) for k in range(dirs)]
        stats[c, 0] = jnp.broadcast_to(s, (tokens, 128))
        for k in range(dirs):
            stats[c, k + 1] = jnp.broadcast_to(u[k], (tokens, 128))
        for half in range(2):
            for j in range(tiles):
                at = pl.ds(j * tile, tile)
                h = whole[c, half, rows(0), at].astype(F32)
                gain = gain_ref[half, :, at]
                n = h * s
                operand[half, rows(0), at] = (n * gain).astype(BF16)
                for k in range(dirs):
                    t = whole[c, half, rows(k + 1), at].astype(F32)
                    mixed = (t * s + h * u[k]) * gain + n * probe_ref[half, k : k + 1, at]
                    operand[half, rows(k + 1), at] = mixed.astype(BF16)

        def product(j, carry):
            at = pl.ds(pl.multiple_of(j * tile, tile), tile)
            a = jnp.dot(operand[0], weight_ref[0, :, at], preferred_element_type=F32)
            a = a + jnp.dot(operand[1], weight_ref[1, :, at], preferred_element_type=F32)
            b = jnp.tanh(a[0:tokens])
            slope = 1.0 - b * b
            act[c, rows(0), at] = b
            out[c, rows(0), at] = (whole[c, core, rows(0), at].astype(F32) + b).astype(BF16)
            for k in range(1, dirs + 1):
                bk = slope * a[k * tokens : (k + 1) * tokens]
                act[c, rows(k), at] = bk
                out[c, rows(k), at] = (whole[c, core, rows(k), at].astype(F32) + bk).astype(BF16)
            return carry

        lax.fori_loop(0, tiles, product, 0)

        @pl.when(pos < last)
        def _():
            hop(c).start()

    def backward(c):
        @pl.when(pos == last)
        def _():
            error = out[c, rows(0), :].astype(F32) - target_ref[c].astype(F32)
            cot_in[c, rows(0), :] = error.astype(BF16)
            cot_in[c, tokens:, :] = out[c, tokens:, :]

        @pl.when(pos < last)
        def _():
            back(c).wait_recv()

        for j in range(tiles):
            at = pl.ds(j * tile, tile)
            c0 = cot_in[c, rows(0), at].astype(F32)
            b = act[c, rows(0), at]
            slope = 1.0 - b * b
            twice = 2.0 * b * c0
            gstack[rows(0), at] = (c0 * slope).astype(BF16)
            for k in range(1, dirs + 1):
                ck = cot_in[c, rows(k), at].astype(F32)
                gstack[rows(k), at] = (ck * slope - twice * act[c, rows(k), at]).astype(BF16)

        s = stats[c, 0, :, 0:1]
        u = [stats[c, k + 1, :, 0:1] for k in range(dirs)]

        def product(j, sums):
            half = j // tiles
            at = pl.ds(pl.multiple_of((j % tiles) * tile, tile), tile)
            q_all = lax.dot_general(
                gstack[...],
                weight_ref[half, at, :],
                (((1,), (1,)), ((), ())),
                preferred_element_type=F32,
            )
            q[half, :, at] = q_all
            h = whole[c, half, rows(0), at].astype(F32)
            gain = gain_ref[half, :, at]
            q0 = q_all[0:tokens]
            n = h * s
            p = q0 * gain
            new = [sums[0] + fold(p * h)]
            for k in range(dirs):
                t = whole[c, half, rows(k + 1), at].astype(F32)
                qk = q_all[(k + 1) * tokens : (k + 2) * tokens]
                v = t * s + h * u[k]
                pk = qk * gain + q0 * probe_ref[half, k : k + 1, at]
                new.append(sums[k + 1] + fold(pk * h + p * t))
                acc_ref[half, k : k + 1, at] += jnp.sum(qk * n + q0 * v, axis=0, keepdims=True)
            return tuple(new)

        zero = jnp.zeros((tokens, 128), F32)
        sums = lax.fori_loop(0, 2 * tiles, product, (zero,) * (dirs + 1))

        @pl.when(pos > 0)
        def _():
            w = [jnp.sum(value, axis=-1, keepdims=True) for value in sums]
            cube = s * s * s / features
            w0 = cube * w[0]
            pull = [(3.0 / features) * s * s * u[k] * w[0] + cube * w[k + 1] for k in range(dirs)]

            def leaving(half, at):
                h = whole[c, half, rows(0), at].astype(F32)
                gain = gain_ref[half, :, at]
                q0 = q[half, rows(0), at]
                p = q0 * gain
                yield s * p - h * w0
                for k in range(dirs):
                    t = whole[c, half, rows(k + 1), at].astype(F32)
                    pk = q[half, rows(k + 1), at] * gain + q0 * probe_ref[half, k : k + 1, at]
                    yield u[k] * p + s * pk - h * pull[k] - t * w0

            for j in range(tiles):
                at = pl.ds(j * tile, tile)
                for k, value in enumerate(leaving(1 - core, at)):
                    part_out[c, rows(k), at] = value.astype(BF16)
            exchange = part(c)
            exchange.start()
            for j in range(tiles):
                at = pl.ds(j * tile, tile)
                for k, value in enumerate(list(leaving(core, at))):
                    q[core, rows(k), at] = value + cot_in[c, rows(k), at].astype(F32)
            exchange.wait_recv()
            for j in range(tiles):
                at = pl.ds(j * tile, tile)
                cot_out[c, :, at] = (q[core, :, at] + part_in[c, :, at].astype(F32)).astype(BF16)
            back(c).start()

    lag = jnp.minimum(lag_step * (last - pos), chunks)

    def turn(i, carry):
        @pl.when(i < chunks)
        def _():
            forward(jnp.minimum(i, chunks - 1))

        @pl.when((i >= lag) & (i - lag < chunks))
        def _():
            backward(jnp.clip(i - lag, 0, chunks - 1))

        return carry

    lax.fori_loop(0, chunks + min(lag_step * last, chunks), turn, 0)

    def drain(c, carry):
        @pl.when(pos < last)
        def _():
            hop(c).wait_send()

        @pl.when(pos > 0)
        def _():
            sibling(c).wait_send()
            part(c).wait_send()
            back(c).wait_send()

        return carry

    lax.fori_loop(0, chunks, drain, 0)


def relay(inputs, target, gain, probe, weight, sections, chunk_tokens, lag_step):
    features = inputs.shape[-1]
    cols = features // 2
    dirs = probe.shape[0]
    chunks = inputs.shape[0] * inputs.shape[1] // chunk_tokens
    height = (dirs + 1) * chunk_tokens
    vmem = pl.BlockSpec(memory_space=pltpu.VMEM)
    dma = pltpu.SemaphoreType.DMA((chunks,))
    acc = pl.pallas_call(
        functools.partial(relay_kernel, sections, lag_step),
        out_shape=jax.ShapeDtypeStruct((2, dirs, cols), F32),
        in_specs=[vmem] * 5,
        out_specs=vmem,
        scratch_shapes=[
            pltpu.VMEM((chunks, 2, height, cols), BF16),
            pltpu.VMEM((chunks, height, cols), F32),
            pltpu.VMEM((chunks, height, cols), BF16),
            pltpu.VMEM((chunks, height, cols), BF16),
            pltpu.VMEM((chunks, height, cols), BF16),
            pltpu.VMEM((chunks, height, cols), BF16),
            pltpu.VMEM((chunks, height, cols), BF16),
            pltpu.VMEM((2, height, cols), BF16),
            pltpu.VMEM((height, cols), BF16),
            pltpu.VMEM((2, height, cols), F32),
            pltpu.VMEM((chunks, dirs + 1, chunk_tokens, 128), F32),
        ]
        + [dma] * 8,
        compiler_params=pltpu.CompilerParams(
            collective_id=0, has_side_effects=True, vmem_limit_bytes=56 * 1024 * 1024
        ),
        cost_estimate=pl.CostEstimate(
            flops=4 * chunks * height * features * cols, bytes_accessed=2 * features * cols, transcendentals=0
        ),
    )(
        inputs.reshape(chunks, chunk_tokens, features),
        target.reshape(chunks, chunk_tokens, cols),
        gain.reshape(2, 1, cols),
        probe.reshape(dirs, 2, cols).transpose(1, 0, 2),
        weight.reshape(2, cols, cols),
    )
    return acc.transpose(1, 0, 2).reshape(dirs, features)


def local(inputs, target, gains, weights, probes):
    sections = lax.axis_size("section")
    batches, micro_batch_tokens, features = inputs.shape
    weight = lax.all_gather(weights, "dp", axis=1, tiled=True)[0]
    probe_dirs = lax.all_gather(probes.astype(BF16), "dp", axis=2, tiled=True).astype(F32)[:, 0, :]
    accumulated = relay(inputs, target, gains[0], probe_dirs, weight, sections, 16, 3)
    divisor = batches * micro_batch_tokens * lax.axis_size("dp")
    own_probe = probes[:, 0, :]
    owned = lax.psum_scatter(
        accumulated.astype(BF16), "dp", scatter_dimension=1, tiled=True
    ).astype(F32)
    owned = lax.psum(owned, "mp")
    curvature = owned / divisor
    moved = own_probe + ETA * curvature
    local_gram = jnp.dot(moved, moved.T, precision=lax.Precision.HIGHEST)
    gram = lax.psum(local_gram, ("dp", "section"))
    factor = jnp.linalg.cholesky(gram)
    rotated = jax.scipy.linalg.solve_triangular(factor, moved, lower=True) * math.sqrt(
        sections * features
    )
    return (curvature[:, None, :], rotated[:, None, :])


def solution(mesh):
    in_specs = (
        P(None, "dp", None),
        P(None, "dp", "mp"),
        P("section", None),
        P("section", "dp", "mp"),
        P(None, "section", "dp"),
    )
    out_specs = (P(None, "section", "dp"), P(None, "section", "dp"))
    return jax.shard_map(local, mesh=mesh, in_specs=in_specs, out_specs=out_specs, check_vma=False)
```

```python
import functools
import math

import jax
import jax.numpy as jnp
from jax import lax
from jax.experimental import pallas as pl
from jax.experimental.pallas import tpu as pltpu
from jax.sharding import PartitionSpec as P

EPS = 1e-05
ETA = 0.5
MESH = pl.DeviceIdType.MESH
F32 = jnp.float32
BF16 = jnp.bfloat16


def fold(values):
    total = values[..., 0:128]
    for start in range(128, values.shape[-1], 128):
        total = total + values[..., start : start + 128]
    return total


def relay_kernel(
    sections,
    lag_step,
    inputs_ref,
    target_ref,
    gain_ref,
    probe_block_ref,
    weight_block_ref,
    acc_ref,
    weight_all,
    probe_all,
    whole,
    act,
    out,
    cot_in,
    cot_out,
    part_out,
    part_in,
    operand,
    gstack,
    q,
    stats,
    hop_send,
    hop_recv,
    sib_send,
    sib_recv,
    part_send,
    part_recv,
    back_send,
    back_recv,
    right_send,
    right_recv,
    left_send,
    left_recv,
    probe_send,
    probe_recv,
    own_sem,
):
    pos = lax.axis_index("section")
    core = lax.axis_index("mp")
    last = sections - 1
    chunks, tokens, features = inputs_ref.shape
    cols = features // 2
    dirs = probe_all.shape[0]
    owners = lax.axis_size("dp")
    me = lax.axis_index("dp")
    depth = weight_block_ref.shape[0]
    width = probe_block_ref.shape[1]
    gather_probes = width < features
    tile = 512 if cols % 512 == 0 else 256 if cols % 256 == 0 else 128
    tiles = cols // tile

    barrier = pltpu.get_barrier_semaphore()
    pl.semaphore_signal(barrier, inc=1, device_id={"mp": 1 - core}, device_id_type=MESH)

    @pl.when(pos > 0)
    def _():
        pl.semaphore_signal(barrier, inc=1, device_id={"section": pos - 1}, device_id_type=MESH)

    @pl.when(pos < last)
    def _():
        pl.semaphore_signal(barrier, inc=1, device_id={"section": pos + 1}, device_id_type=MESH)

    def block_rows(b):
        return pl.ds(pl.multiple_of(b * depth, depth), depth)

    def greet(step, carry):
        peer = lax.rem(me + step, owners)
        pl.semaphore_signal(barrier, inc=1, device_id={"dp": peer}, device_id_type=MESH)
        return carry

    lax.fori_loop(1, owners, greet, 0)
    own = pltpu.make_async_copy(weight_block_ref, weight_all.at[block_rows(me)], own_sem)
    own.start()
    peers = owners + (pos > 0).astype(jnp.int32) + (pos < last).astype(jnp.int32)
    pl.semaphore_wait(barrier, peers)
    own.wait()

    def to_right(b):
        return pltpu.make_async_remote_copy(
            src_ref=weight_all.at[block_rows(b)],
            dst_ref=weight_all.at[block_rows(b)],
            send_sem=right_send.at[b],
            recv_sem=right_recv.at[b],
            device_id={"dp": me + 1},
            device_id_type=MESH,
        )

    def to_left(b):
        return pltpu.make_async_remote_copy(
            src_ref=weight_all.at[block_rows(b)],
            dst_ref=weight_all.at[block_rows(b)],
            send_sem=left_send.at[b],
            recv_sem=left_recv.at[b],
            device_id={"dp": me - 1},
            device_id_type=MESH,
        )

    @pl.when(me < owners - 1)
    def _():
        to_right(me).start()

    @pl.when(me > 0)
    def _():
        to_left(me).start()

    def probe_to(step):
        mine = pl.ds(pl.multiple_of(me * width, width), width)
        return pltpu.make_async_remote_copy(
            src_ref=probe_all.at[:, mine],
            dst_ref=probe_all.at[:, mine],
            send_sem=probe_send.at[step],
            recv_sem=probe_recv.at[step],
            device_id={"dp": lax.rem(me + step, owners)},
            device_id_type=MESH,
        )

    if gather_probes:
        probe_all[:, pl.ds(pl.multiple_of(me * width, width), width)] = probe_block_ref[...]

        def spread(step, carry):
            probe_to(step).start()
            return carry

        lax.fori_loop(1, owners, spread, 0)
    else:
        probe_all[...] = probe_block_ref[...]

    def hop(c):
        return pltpu.make_async_remote_copy(
            src_ref=out.at[c],
            dst_ref=whole.at[c, core],
            send_sem=hop_send.at[c],
            recv_sem=hop_recv.at[c],
            device_id={"section": pos + 1},
            device_id_type=MESH,
        )

    def sibling(c):
        return pltpu.make_async_remote_copy(
            src_ref=whole.at[c, core],
            dst_ref=whole.at[c, core],
            send_sem=sib_send.at[c],
            recv_sem=sib_recv.at[c],
            device_id={"mp": 1 - core},
            device_id_type=MESH,
        )

    def part(c):
        return pltpu.make_async_remote_copy(
            src_ref=part_out.at[c],
            dst_ref=part_in.at[c],
            send_sem=part_send.at[c],
            recv_sem=part_recv.at[c],
            device_id={"mp": 1 - core},
            device_id_type=MESH,
        )

    def back(c):
        return pltpu.make_async_remote_copy(
            src_ref=cot_out.at[c],
            dst_ref=cot_in.at[c],
            send_sem=back_send.at[c],
            recv_sem=back_recv.at[c],
            device_id={"section": pos - 1},
            device_id_type=MESH,
        )

    def probe_at(half, k, at):
        start = half * cols + at.start
        if not isinstance(start, int):
            start = pl.multiple_of(start, 128)
        return probe_all[k : k + 1, pl.ds(start, tile)]

    def rows(k):
        return pl.ds(k * tokens, tokens)

    acc_ref[...] = jnp.zeros_like(acc_ref)

    def relay_blocks(step, carry):
        low, high = me - step, me + step

        @pl.when(low >= 0)
        def _():
            to_right(low).wait_recv()

            @pl.when(me < owners - 1)
            def _():
                to_right(low).start()

        @pl.when(high < owners)
        def _():
            to_left(high).wait_recv()

            @pl.when(me > 0)
            def _():
                to_left(high).start()

        return carry

    lax.fori_loop(1, owners, relay_blocks, 0)
    if gather_probes:

        def probes_in(step, carry):
            probe_to(step).wait_recv()
            return carry

        lax.fori_loop(1, owners, probes_in, 0)

    def forward(c):
        @pl.when(pos == 0)
        def _():
            for half in range(2):
                whole[c, half, 0:tokens, :] = inputs_ref[c, :, half * cols : (half + 1) * cols]
                whole[c, half, tokens:, :] = jnp.zeros((dirs * tokens, cols), BF16)

        @pl.when(pos > 0)
        def _():
            hop(c).wait_recv()
            swap = sibling(c)
            swap.start()
            swap.wait_recv()

        square = jnp.zeros((tokens, 128), F32)
        cross = [jnp.zeros((tokens, 128), F32) for _ in range(dirs)]
        for half in range(2):
            for j in range(tiles):
                at = pl.ds(j * tile, tile)
                h = whole[c, half, rows(0), at].astype(F32)
                square = square + fold(h * h)
                for k in range(dirs):
                    cross[k] = cross[k] + fold(h * whole[c, half, rows(k + 1), at].astype(F32))
        s = lax.rsqrt(jnp.sum(square, axis=-1, keepdims=True) / features + EPS)
        cube = -(s * s * s) / features
        u = [cube * jnp.sum(cross[k], axis=-1, keepdims=True) for k in range(dirs)]
        stats[c, 0] = jnp.broadcast_to(s, (tokens, 128))
        for k in range(dirs):
            stats[c, k + 1] = jnp.broadcast_to(u[k], (tokens, 128))
        for half in range(2):
            for j in range(tiles):
                at = pl.ds(j * tile, tile)
                h = whole[c, half, rows(0), at].astype(F32)
                gain = gain_ref[half, :, at]
                n = h * s
                operand[half, rows(0), at] = (n * gain).astype(BF16)
                for k in range(dirs):
                    t = whole[c, half, rows(k + 1), at].astype(F32)
                    mixed = (t * s + h * u[k]) * gain + n * probe_at(half, k, at)
                    operand[half, rows(k + 1), at] = mixed.astype(BF16)

        def product(j, carry):
            at = pl.ds(pl.multiple_of(j * tile, tile), tile)
            a = jnp.dot(operand[0], weight_all[0:cols, at], preferred_element_type=F32)
            a = a + jnp.dot(operand[1], weight_all[cols:, at], preferred_element_type=F32)
            b = jnp.tanh(a[0:tokens])
            slope = 1.0 - b * b
            act[c, rows(0), at] = b
            out[c, rows(0), at] = (whole[c, core, rows(0), at].astype(F32) + b).astype(BF16)
            for k in range(1, dirs + 1):
                bk = slope * a[k * tokens : (k + 1) * tokens]
                act[c, rows(k), at] = bk
                out[c, rows(k), at] = (whole[c, core, rows(k), at].astype(F32) + bk).astype(BF16)
            return carry

        lax.fori_loop(0, tiles, product, 0)

        @pl.when(pos < last)
        def _():
            hop(c).start()

    def backward(c):
        @pl.when(pos == last)
        def _():
            error = out[c, rows(0), :].astype(F32) - target_ref[c].astype(F32)
            cot_in[c, rows(0), :] = error.astype(BF16)
            cot_in[c, tokens:, :] = out[c, tokens:, :]

        @pl.when(pos < last)
        def _():
            back(c).wait_recv()

        for j in range(tiles):
            at = pl.ds(j * tile, tile)
            c0 = cot_in[c, rows(0), at].astype(F32)
            b = act[c, rows(0), at]
            slope = 1.0 - b * b
            twice = 2.0 * b * c0
            gstack[rows(0), at] = (c0 * slope).astype(BF16)
            for k in range(1, dirs + 1):
                ck = cot_in[c, rows(k), at].astype(F32)
                gstack[rows(k), at] = (ck * slope - twice * act[c, rows(k), at]).astype(BF16)

        s = stats[c, 0, :, 0:1]
        u = [stats[c, k + 1, :, 0:1] for k in range(dirs)]

        def product(j, sums):
            half = j // tiles
            at = pl.ds(pl.multiple_of((j % tiles) * tile, tile), tile)
            q_all = lax.dot_general(
                gstack[...],
                weight_all[pl.ds(pl.multiple_of(j * tile, tile), tile), :],
                (((1,), (1,)), ((), ())),
                preferred_element_type=F32,
            )
            q[half, :, at] = q_all
            h = whole[c, half, rows(0), at].astype(F32)
            gain = gain_ref[half, :, at]
            q0 = q_all[0:tokens]
            n = h * s
            p = q0 * gain
            new = [sums[0] + fold(p * h)]
            for k in range(dirs):
                t = whole[c, half, rows(k + 1), at].astype(F32)
                qk = q_all[(k + 1) * tokens : (k + 2) * tokens]
                v = t * s + h * u[k]
                pk = qk * gain + q0 * probe_at(half, k, at)
                new.append(sums[k + 1] + fold(pk * h + p * t))
                acc_ref[half, k : k + 1, at] += jnp.sum(qk * n + q0 * v, axis=0, keepdims=True)
            return tuple(new)

        zero = jnp.zeros((tokens, 128), F32)
        sums = lax.fori_loop(0, 2 * tiles, product, (zero,) * (dirs + 1))

        @pl.when(pos > 0)
        def _():
            w = [jnp.sum(value, axis=-1, keepdims=True) for value in sums]
            cube = s * s * s / features
            w0 = cube * w[0]
            pull = [(3.0 / features) * s * s * u[k] * w[0] + cube * w[k + 1] for k in range(dirs)]

            def leaving(half, at):
                h = whole[c, half, rows(0), at].astype(F32)
                gain = gain_ref[half, :, at]
                q0 = q[half, rows(0), at]
                p = q0 * gain
                yield s * p - h * w0
                for k in range(dirs):
                    t = whole[c, half, rows(k + 1), at].astype(F32)
                    pk = q[half, rows(k + 1), at] * gain + q0 * probe_at(half, k, at)
                    yield u[k] * p + s * pk - h * pull[k] - t * w0

            for j in range(tiles):
                at = pl.ds(j * tile, tile)
                for k, value in enumerate(leaving(1 - core, at)):
                    part_out[c, rows(k), at] = value.astype(BF16)
            exchange = part(c)
            exchange.start()
            for j in range(tiles):
                at = pl.ds(j * tile, tile)
                for k, value in enumerate(list(leaving(core, at))):
                    q[core, rows(k), at] = value + cot_in[c, rows(k), at].astype(F32)
            exchange.wait_recv()
            for j in range(tiles):
                at = pl.ds(j * tile, tile)
                cot_out[c, :, at] = (q[core, :, at] + part_in[c, :, at].astype(F32)).astype(BF16)
            back(c).start()

    lag = jnp.minimum(lag_step * (last - pos), chunks)

    def turn(i, carry):
        @pl.when(i < chunks)
        def _():
            forward(jnp.minimum(i, chunks - 1))

        @pl.when((i >= lag) & (i - lag < chunks))
        def _():
            backward(jnp.clip(i - lag, 0, chunks - 1))

        return carry

    lax.fori_loop(0, chunks + min(lag_step * last, chunks), turn, 0)

    def drain(c, carry):
        @pl.when(pos < last)
        def _():
            hop(c).wait_send()

        @pl.when(pos > 0)
        def _():
            sibling(c).wait_send()
            part(c).wait_send()
            back(c).wait_send()

        return carry

    lax.fori_loop(0, chunks, drain, 0)

    def drain_blocks(b, carry):
        @pl.when((me < owners - 1) & (b <= me))
        def _():
            to_right(b).wait_send()

        @pl.when((me > 0) & (b >= me))
        def _():
            to_left(b).wait_send()

        return carry

    lax.fori_loop(0, owners, drain_blocks, 0)
    if gather_probes:

        def drain_probes(step, carry):
            probe_to(step).wait_send()
            return carry

        lax.fori_loop(1, owners, drain_probes, 0)


def settle_kernel(scale, divisor, parts_ref, probe_ref, hvp_ref, next_ref, got, tiles, sends, recvs, tile_sends, tile_recvs):
    owners, dirs, width = parts_ref.shape
    sections = lax.axis_size("section")
    dp, pos, core = lax.axis_index("dp"), lax.axis_index("section"), lax.axis_index("mp")
    pairs = [(i, j) for i in range(dirs) for j in range(i + 1)]
    group = 2 * owners
    everyone = owners * sections
    me = dp * 2 + core
    place = dp * sections + pos

    barrier = pltpu.get_barrier_semaphore()

    def greet_owner(step, carry):
        peer = lax.rem(me + step, group)
        target = {"dp": peer // 2, "mp": lax.rem(peer, 2)}
        pl.semaphore_signal(barrier, inc=1, device_id=target, device_id_type=MESH)
        return carry

    def greet_other(step, carry):
        target = {"dp": lax.rem(step, owners), "section": lax.rem(pos + 1 + step // owners, sections)}
        pl.semaphore_signal(barrier, inc=1, device_id=target, device_id_type=MESH)
        return carry

    lax.fori_loop(1, group, greet_owner, 0)
    lax.fori_loop(0, owners * (sections - 1), greet_other, 0)
    pl.semaphore_wait(barrier, group - 1 + owners * (sections - 1))

    def give(step):
        peer = lax.rem(me + step, group)
        return pltpu.make_async_remote_copy(
            src_ref=parts_ref.at[peer // 2],
            dst_ref=got.at[step],
            send_sem=sends.at[step],
            recv_sem=recvs.at[step],
            device_id={"dp": peer // 2, "mp": lax.rem(peer, 2)},
            device_id_type=MESH,
        )

    def start_give(step, carry):
        give(step).start()
        return carry

    lax.fori_loop(1, group, start_give, 0)

    def take(step, total):
        give(step).wait_recv()
        return total + got[step]

    curvature = lax.fori_loop(1, group, take, parts_ref[dp]) / divisor
    hvp_ref[...] = curvature
    moved = probe_ref[...] + ETA * curvature
    row = lax.broadcasted_iota(jnp.int32, (16, 128), 0)
    tile = jnp.zeros((16, 128), F32)
    for index, (i, j) in enumerate(pairs):
        inner = jnp.sum(moved[i : i + 1] * moved[j : j + 1], axis=1, keepdims=True)
        tile = jnp.where(row == index, inner, tile)
    tiles[0] = tile

    def tell(step):
        peer = lax.rem(place + step, everyone)
        return pltpu.make_async_remote_copy(
            src_ref=tiles.at[0],
            dst_ref=tiles.at[step],
            send_sem=tile_sends.at[step],
            recv_sem=tile_recvs.at[step],
            device_id={"dp": peer // sections, "section": lax.rem(peer, sections)},
            device_id_type=MESH,
        )

    def start_tell(step, carry):
        tell(step).start()
        return carry

    lax.fori_loop(1, everyone, start_tell, 0)

    def hear(step, carry):
        tell(step).wait_recv()
        return carry

    lax.fori_loop(1, everyone, hear, 0)
    gram = lax.fori_loop(
        0,
        everyone,
        lambda source, total: total + tiles[lax.rem(place - source + everyone, everyone)],
        jnp.zeros((16, 128), F32),
    )
    entry = {pair: gram[index : index + 1, 0:1] for index, pair in enumerate(pairs)}
    factor = {}
    for j in range(dirs):
        rest = entry[j, j]
        for k in range(j):
            rest = rest - factor[j, k] * factor[j, k]
        factor[j, j] = jnp.sqrt(rest)
        for i in range(j + 1, dirs):
            rest = entry[i, j]
            for k in range(j):
                rest = rest - factor[i, k] * factor[j, k]
            factor[i, j] = rest / factor[j, j]
    solved = []
    for i in range(dirs):
        value = moved[i : i + 1]
        for k in range(i):
            value = value - factor[i, k] * solved[k]
        solved.append(value / factor[i, i])
        next_ref[i : i + 1, :] = solved[i] * scale

    def drain_give(step, carry):
        give(step).wait_send()
        return carry

    def drain_tell(step, carry):
        tell(step).wait_send()
        return carry

    lax.fori_loop(1, group, drain_give, 0)
    lax.fori_loop(1, everyone, drain_tell, 0)


def settle(accumulated, own_probe, scale, divisor):
    dirs, width = own_probe.shape
    owners, sections = lax.axis_size("dp"), lax.axis_size("section")
    vmem = pl.BlockSpec(memory_space=pltpu.VMEM)
    return pl.pallas_call(
        functools.partial(settle_kernel, scale, divisor),
        out_shape=[jax.ShapeDtypeStruct((dirs, width), F32)] * 2,
        in_specs=[vmem] * 2,
        out_specs=[vmem] * 2,
        scratch_shapes=[
            pltpu.VMEM((2 * owners, dirs, width), F32),
            pltpu.VMEM((owners * sections, 16, 128), F32),
        ]
        + [pltpu.SemaphoreType.DMA((2 * owners,))] * 2
        + [pltpu.SemaphoreType.DMA((owners * sections,))] * 2,
        compiler_params=pltpu.CompilerParams(
            collective_id=1, has_side_effects=True, vmem_limit_bytes=16 * 1024 * 1024
        ),
    )(accumulated.reshape(dirs, owners, width).transpose(1, 0, 2), own_probe)


def relay(inputs, target, gain, probe, weight, sections, chunk_tokens, lag_step):
    features = inputs.shape[-1]
    cols = features // 2
    dirs = probe.shape[0]
    chunks = inputs.shape[0] * inputs.shape[1] // chunk_tokens
    height = (dirs + 1) * chunk_tokens
    vmem = pl.BlockSpec(memory_space=pltpu.VMEM)
    dma = pltpu.SemaphoreType.DMA((chunks,))
    ring = pltpu.SemaphoreType.DMA((lax.axis_size("dp"),))
    acc = pl.pallas_call(
        functools.partial(relay_kernel, sections, lag_step),
        out_shape=jax.ShapeDtypeStruct((2, dirs, cols), F32),
        in_specs=[vmem] * 4 + [pl.BlockSpec(memory_space=pl.ANY)],
        out_specs=vmem,
        scratch_shapes=[
            pltpu.VMEM((features, cols), BF16),
            pltpu.VMEM((dirs, features), F32),
            pltpu.VMEM((chunks, 2, height, cols), BF16),
            pltpu.VMEM((chunks, height, cols), F32),
            pltpu.VMEM((chunks, height, cols), BF16),
            pltpu.VMEM((chunks, height, cols), BF16),
            pltpu.VMEM((chunks, height, cols), BF16),
            pltpu.VMEM((chunks, height, cols), BF16),
            pltpu.VMEM((chunks, height, cols), BF16),
            pltpu.VMEM((2, height, cols), BF16),
            pltpu.VMEM((height, cols), BF16),
            pltpu.VMEM((2, height, cols), F32),
            pltpu.VMEM((chunks, dirs + 1, chunk_tokens, 128), F32),
        ]
        + [dma] * 8
        + [ring] * 6
        + [pltpu.SemaphoreType.DMA],
        compiler_params=pltpu.CompilerParams(
            collective_id=0, has_side_effects=True, vmem_limit_bytes=56 * 1024 * 1024
        ),
        cost_estimate=pl.CostEstimate(
            flops=4 * chunks * height * features * cols, bytes_accessed=2 * features * cols, transcendentals=0
        ),
    )(
        inputs.reshape(chunks, chunk_tokens, features),
        target.reshape(chunks, chunk_tokens, cols),
        gain.reshape(2, 1, cols),
        probe,
        weight,
    )
    return acc.transpose(1, 0, 2).reshape(dirs, features)


def local(inputs, target, gains, weights, probes):
    sections = lax.axis_size("section")
    batches, micro_batch_tokens, features = inputs.shape
    probe_block = probes[:, 0, :]
    if probe_block.shape[1] % 128:
        probe_block = lax.all_gather(probe_block, "dp", axis=1, tiled=True)
    accumulated = relay(inputs, target, gains[0], probe_block, weights[0], sections, 16, 3)
    divisor = batches * micro_batch_tokens * lax.axis_size("dp")
    curvature, rotated = settle(accumulated, probes[:, 0, :], math.sqrt(sections * features), divisor)
    return (curvature[:, None, :], rotated[:, None, :])


def solution(mesh):
    in_specs = (
        P(None, "dp", None),
        P(None, "dp", "mp"),
        P("section", None),
        P("section", "dp", "mp"),
        P(None, "section", "dp"),
    )
    out_specs = (P(None, "section", "dp"), P(None, "section", "dp"))
    return jax.shard_map(local, mesh=mesh, in_specs=in_specs, out_specs=out_specs, check_vma=False)
```

```python
import functools
import math

import jax
import jax.numpy as jnp
from jax import lax
from jax.experimental import pallas as pl
from jax.experimental.pallas import tpu as pltpu
from jax.sharding import PartitionSpec as P

EPS = 1e-05
ETA = 0.5
MESH = pl.DeviceIdType.MESH
F32 = jnp.float32
BF16 = jnp.bfloat16


def fold(values):
    total = values[..., 0:128]
    for start in range(128, values.shape[-1], 128):
        total = total + values[..., start : start + 128]
    return total


def straight_gather(pos, last, core, weight_block_ref, weight_all, probe_block_ref, probe_all, right_send, right_recv, left_send, left_recv, probe_send, probe_recv, own_sem):
    owners = lax.axis_size("dp")
    me = lax.axis_index("dp")
    depth = weight_block_ref.shape[0]
    width = probe_block_ref.shape[1]
    gather_probes = width < probe_all.shape[1]

    barrier = pltpu.get_barrier_semaphore()
    pl.semaphore_signal(barrier, inc=1, device_id={"mp": 1 - core}, device_id_type=MESH)

    @pl.when(pos > 0)
    def _():
        pl.semaphore_signal(barrier, inc=1, device_id={"section": pos - 1}, device_id_type=MESH)

    @pl.when(pos < last)
    def _():
        pl.semaphore_signal(barrier, inc=1, device_id={"section": pos + 1}, device_id_type=MESH)

    def block_rows(b):
        return pl.ds(pl.multiple_of(b * depth, depth), depth)

    def greet(step, carry):
        peer = lax.rem(me + step, owners)
        pl.semaphore_signal(barrier, inc=1, device_id={"dp": peer}, device_id_type=MESH)
        return carry

    lax.fori_loop(1, owners, greet, 0)
    own = pltpu.make_async_copy(weight_block_ref, weight_all.at[block_rows(me)], own_sem)
    own.start()
    peers = owners + (pos > 0).astype(jnp.int32) + (pos < last).astype(jnp.int32)
    pl.semaphore_wait(barrier, peers)
    own.wait()

    def to_right(b):
        return pltpu.make_async_remote_copy(
            src_ref=weight_all.at[block_rows(b)],
            dst_ref=weight_all.at[block_rows(b)],
            send_sem=right_send.at[b],
            recv_sem=right_recv.at[b],
            device_id={"dp": me + 1},
            device_id_type=MESH,
        )

    def to_left(b):
        return pltpu.make_async_remote_copy(
            src_ref=weight_all.at[block_rows(b)],
            dst_ref=weight_all.at[block_rows(b)],
            send_sem=left_send.at[b],
            recv_sem=left_recv.at[b],
            device_id={"dp": me - 1},
            device_id_type=MESH,
        )

    @pl.when(me < owners - 1)
    def _():
        to_right(me).start()

    @pl.when(me > 0)
    def _():
        to_left(me).start()

    def probe_to(step):
        mine = pl.ds(pl.multiple_of(me * width, width), width)
        return pltpu.make_async_remote_copy(
            src_ref=probe_all.at[:, mine],
            dst_ref=probe_all.at[:, mine],
            send_sem=probe_send.at[step],
            recv_sem=probe_recv.at[step],
            device_id={"dp": lax.rem(me + step, owners)},
            device_id_type=MESH,
        )

    if gather_probes:
        probe_all[:, pl.ds(pl.multiple_of(me * width, width), width)] = probe_block_ref[...]

        def spread(step, carry):
            probe_to(step).start()
            return carry

        lax.fori_loop(1, owners, spread, 0)
    else:
        probe_all[...] = probe_block_ref[...]


    def relay_blocks(step, carry):
        low, high = me - step, me + step

        @pl.when(low >= 0)
        def _():
            to_right(low).wait_recv()

            @pl.when(me < owners - 1)
            def _():
                to_right(low).start()

        @pl.when(high < owners)
        def _():
            to_left(high).wait_recv()

            @pl.when(me > 0)
            def _():
                to_left(high).start()

        return carry

    lax.fori_loop(1, owners, relay_blocks, 0)
    if gather_probes:

        def probes_in(step, carry):
            probe_to(step).wait_recv()
            return carry

        lax.fori_loop(1, owners, probes_in, 0)


    def drain():
        def drain_blocks(b, carry):
            @pl.when((me < owners - 1) & (b <= me))
            def _():
                to_right(b).wait_send()

            @pl.when((me > 0) & (b >= me))
            def _():
                to_left(b).wait_send()

            return carry

        lax.fori_loop(0, owners, drain_blocks, 0)
        if gather_probes:

            def drain_probes(step, carry):
                probe_to(step).wait_send()
                return carry

            lax.fori_loop(1, owners, drain_probes, 0)

    return drain


def crossed_gather(
    inputs_arg, target_arg, gain_arg, probe_block_ref, weight_block_ref, weight_all, probe_all,
    inputs_buf, target_buf, gain_buf, stage, sems, local_sems, one_sems,
):
    owners = lax.axis_size("dp")
    plane, column, core = lax.axis_index("dp"), lax.axis_index("section"), lax.axis_index("mp")
    depth = weight_block_ref.shape[0]
    piece = depth // owners
    width = probe_block_ref.shape[1]
    place = plane * owners + column
    out_send, out_recv, up_send, up_recv, x_send, x_recv, y_send, y_recv = [sems.at[i] for i in range(8)]
    fx_send, fx_recv, fy_send, fy_recv, probe_send, probe_recv, gain_send = [sems.at[i] for i in range(8, 15)]

    def flip(value, bits):
        for bit in (1, 2):
            if bits & bit:
                value = value + bit - 2 * bit * (value // bit % 2)
        return value

    barrier = pltpu.get_barrier_semaphore()

    def greet(step, carry):
        peer = lax.rem(place + step, owners * owners)
        target = {"dp": peer // owners, "section": lax.rem(peer, owners)}
        pl.semaphore_signal(barrier, inc=1, device_id=target, device_id_type=MESH)
        return carry

    lax.fori_loop(1, owners * owners, greet, 0)
    pl.semaphore_signal(barrier, inc=1, device_id={"mp": 1 - core}, device_id_type=MESH)
    pl.semaphore_wait(barrier, owners * owners)

    def remote(src, dst, send, recv, **target):
        return pltpu.make_async_remote_copy(
            src_ref=src, dst_ref=dst, send_sem=send, recv_sem=recv, device_id=target, device_id_type=MESH
        )

    def rows_of(k, t, start=0, count=piece):
        return weight_all.at[pl.ds(pl.multiple_of(k * depth + t * piece + start, 16), count)]

    def out(t):
        src = weight_block_ref.at[pl.ds(pl.multiple_of(t * piece, 16), piece)]
        return remote(src, stage.at[column], out_send.at[t], out_recv.at[column], section=t)

    def out_in(s):
        return remote(stage.at[s], stage.at[s], out_send.at[s], out_recv.at[s], section=s)

    def up(r):
        return remote(stage.at[r], rows_of(plane, column), up_send.at[r], up_recv.at[plane], dp=r)

    def up_in(k):
        return remote(stage.at[k], rows_of(k, column), up_send.at[k], up_recv.at[k], dp=k)

    half = piece // 2
    near_x, near_y, far = flip(column, 1), flip(column, 2), flip(column, 3)

    def to_x(k, t):
        return remote(rows_of(k, t), rows_of(k, t), x_send.at[k], x_recv.at[k], section=near_x)

    def to_y(k, t):
        return remote(rows_of(k, t), rows_of(k, t), y_send.at[k], y_recv.at[k], section=near_y)

    def on_x(k, t):
        rows = rows_of(k, t, half, half)
        return remote(rows, rows, fx_send.at[k], fx_recv.at[k], section=near_x)

    def on_y(k, t):
        rows = rows_of(k, t, 0, half)
        return remote(rows, rows, fy_send.at[k], fy_recv.at[k], section=near_y)

    first_stage = pltpu.make_async_copy(
        weight_block_ref.at[pl.ds(pl.multiple_of(column * piece, 16), piece)], stage.at[column], local_sems.at[0]
    )
    keep = pltpu.make_async_copy(stage.at[plane], rows_of(plane, column), local_sems.at[1])
    for bits in (3, 1, 2):
        out(flip(column, bits)).start()
    first_stage.start()

    def give_probe(t):
        mine = probe_all.at[:, pl.ds(pl.multiple_of(plane * width, 128), width)]
        return remote(probe_block_ref, mine, probe_send.at[t], probe_recv.at[plane], dp=column, section=t)

    def take_probe(k):
        mine = probe_all.at[:, pl.ds(pl.multiple_of(k * width, 128), width)]
        return remote(probe_block_ref, mine, probe_send.at[k], probe_recv.at[k], dp=k, section=plane)

    def give_gain(t):
        return remote(gain_arg, gain_buf, gain_send.at[t], one_sems.at[0], section=t)

    give_inputs = remote(inputs_arg, inputs_buf, one_sems.at[1], one_sems.at[2], dp=0)
    give_target = remote(target_arg, target_buf, one_sems.at[3], one_sems.at[4], dp=owners - 1)
    diagonal = plane == column
    for t in range(owners):

        @pl.when(~(diagonal & (column == t)))
        def _():
            give_probe(t).start()

        @pl.when(diagonal & (column != t))
        def _():
            give_gain(t).start()

    @pl.when(diagonal)
    def _():
        probe_all[:, pl.ds(pl.multiple_of(plane * width, 128), width)] = probe_block_ref[...]
        gain_buf[...] = gain_arg[...]

    @pl.when(diagonal & (plane != 0))
    def _():
        give_inputs.start()

    @pl.when(diagonal & (plane == 0))
    def _():
        inputs_buf[...] = inputs_arg[...]

    @pl.when(diagonal & (plane != owners - 1))
    def _():
        give_target.start()

    @pl.when(diagonal & (plane == owners - 1))
    def _():
        target_buf[...] = target_arg[...]

    def move_up(s):
        @pl.when(s != plane)
        def _():
            up(s).start()

        @pl.when(s == plane)
        def _():
            keep.start()

    first_stage.wait()
    move_up(column)
    for bits in (1, 2, 3):
        s = flip(column, bits)
        out_in(s).wait_recv()
        move_up(s)

    def pass_on(k):
        to_x(k, near_x).wait_recv()
        on_y(k, near_x).start()
        to_y(k, near_y).wait_recv()
        on_x(k, near_y).start()

    steps = [0]
    for d in range(1, owners):
        steps += [d, -d]

    def when_valid(d, body):
        k = plane + d

        @pl.when((k >= 0) & (k < owners))
        def _():
            body(k)

    def launch(k):
        to_x(k, column).start()
        to_y(k, column).start()

    for index, d in enumerate(steps):
        if d == 0:
            keep.wait()
            launch(plane)
        else:

            def arrive(k):
                up_in(k).wait_recv()
                launch(k)

            when_valid(d, arrive)
        if index > 0:
            when_valid(steps[index - 1], pass_on)
    when_valid(steps[-1], pass_on)
    for k in range(owners):
        on_x(k, far).wait_recv()
        on_y(k, far).wait_recv()

        @pl.when(~(diagonal & (plane == k)))
        def _():
            take_probe(k).wait_recv()

    @pl.when(~diagonal)
    def _():
        give_gain(column).wait_recv()

    @pl.when((plane == 0) & (column != 0))
    def _():
        give_inputs.wait_recv()

    @pl.when((plane == owners - 1) & (column != owners - 1))
    def _():
        give_target.wait_recv()

    def drain():
        for k in range(owners):
            to_x(k, column).wait_send()
            to_y(k, column).wait_send()
            on_x(k, near_y).wait_send()
            on_y(k, near_x).wait_send()

            @pl.when(column != k)
            def _():
                out(k).wait_send()

            @pl.when(plane != k)
            def _():
                up(k).wait_send()

            @pl.when(~(diagonal & (column == k)))
            def _():
                give_probe(k).wait_send()

            @pl.when(diagonal & (column != k))
            def _():
                give_gain(k).wait_send()

        @pl.when(diagonal & (plane != 0))
        def _():
            give_inputs.wait_send()

        @pl.when(diagonal & (plane != owners - 1))
        def _():
            give_target.wait_send()

    return drain


def relay_kernel(
    sections,
    lag_step,
    crossed,
    inputs_arg,
    target_arg,
    gain_arg,
    probe_block_ref,
    weight_block_ref,
    acc_ref,
    weight_all,
    probe_all,
    whole,
    act,
    out,
    cot_in,
    cot_out,
    part_out,
    part_in,
    operand,
    gstack,
    q,
    stats,
    hop_send,
    hop_recv,
    sib_send,
    sib_recv,
    part_send,
    part_recv,
    back_send,
    back_recv,
    right_send,
    right_recv,
    left_send,
    left_recv,
    probe_send,
    probe_recv,
    own_sem,
    *crossed_scratch,
):
    pipe = "dp" if crossed else "section"
    pos = lax.axis_index(pipe)
    core = lax.axis_index("mp")
    last = sections - 1
    chunks, tokens, features = inputs_arg.shape
    if crossed:
        inputs_ref, target_ref, gain_ref = crossed_scratch[:3]
    else:
        inputs_ref, target_ref, gain_ref = inputs_arg, target_arg, gain_arg
    cols = features // 2
    dirs = probe_all.shape[0]
    tile = 512 if cols % 512 == 0 else 256 if cols % 256 == 0 else 128
    tiles = cols // tile

    def hop(c):
        return pltpu.make_async_remote_copy(
            src_ref=out.at[c],
            dst_ref=whole.at[c, core],
            send_sem=hop_send.at[c],
            recv_sem=hop_recv.at[c],
            device_id={pipe: pos + 1},
            device_id_type=MESH,
        )

    def sibling(c):
        return pltpu.make_async_remote_copy(
            src_ref=whole.at[c, core],
            dst_ref=whole.at[c, core],
            send_sem=sib_send.at[c],
            recv_sem=sib_recv.at[c],
            device_id={"mp": 1 - core},
            device_id_type=MESH,
        )

    def part(c):
        return pltpu.make_async_remote_copy(
            src_ref=part_out.at[c],
            dst_ref=part_in.at[c],
            send_sem=part_send.at[c],
            recv_sem=part_recv.at[c],
            device_id={"mp": 1 - core},
            device_id_type=MESH,
        )

    def back(c):
        return pltpu.make_async_remote_copy(
            src_ref=cot_out.at[c],
            dst_ref=cot_in.at[c],
            send_sem=back_send.at[c],
            recv_sem=back_recv.at[c],
            device_id={pipe: pos - 1},
            device_id_type=MESH,
        )

    def probe_at(half, k, at):
        start = half * cols + at.start
        if not isinstance(start, int):
            start = pl.multiple_of(start, 128)
        return probe_all[k : k + 1, pl.ds(start, tile)]

    def rows(k):
        return pl.ds(k * tokens, tokens)

    acc_ref[...] = jnp.zeros_like(acc_ref)

    if crossed:
        drain_gather = crossed_gather(
            inputs_arg, target_arg, gain_arg, probe_block_ref, weight_block_ref, weight_all, probe_all, *crossed_scratch
        )
    else:
        drain_gather = straight_gather(
            pos, last, core, weight_block_ref, weight_all, probe_block_ref, probe_all,
            right_send, right_recv, left_send, left_recv, probe_send, probe_recv, own_sem,
        )

    def forward(c):
        @pl.when(pos == 0)
        def _():
            for half in range(2):
                whole[c, half, 0:tokens, :] = inputs_ref[c, :, half * cols : (half + 1) * cols]
                whole[c, half, tokens:, :] = jnp.zeros((dirs * tokens, cols), BF16)

        @pl.when(pos > 0)
        def _():
            hop(c).wait_recv()
            swap = sibling(c)
            swap.start()
            swap.wait_recv()

        square = jnp.zeros((tokens, 128), F32)
        cross = [jnp.zeros((tokens, 128), F32) for _ in range(dirs)]
        for half in range(2):
            for j in range(tiles):
                at = pl.ds(j * tile, tile)
                h = whole[c, half, rows(0), at].astype(F32)
                square = square + fold(h * h)
                for k in range(dirs):
                    cross[k] = cross[k] + fold(h * whole[c, half, rows(k + 1), at].astype(F32))
        s = lax.rsqrt(jnp.sum(square, axis=-1, keepdims=True) / features + EPS)
        cube = -(s * s * s) / features
        u = [cube * jnp.sum(cross[k], axis=-1, keepdims=True) for k in range(dirs)]
        stats[c, 0] = jnp.broadcast_to(s, (tokens, 128))
        for k in range(dirs):
            stats[c, k + 1] = jnp.broadcast_to(u[k], (tokens, 128))
        for half in range(2):
            for j in range(tiles):
                at = pl.ds(j * tile, tile)
                h = whole[c, half, rows(0), at].astype(F32)
                gain = gain_ref[half, :, at]
                n = h * s
                operand[half, rows(0), at] = (n * gain).astype(BF16)
                for k in range(dirs):
                    t = whole[c, half, rows(k + 1), at].astype(F32)
                    mixed = (t * s + h * u[k]) * gain + n * probe_at(half, k, at)
                    operand[half, rows(k + 1), at] = mixed.astype(BF16)

        def product(j, carry):
            at = pl.ds(pl.multiple_of(j * tile, tile), tile)
            a = jnp.dot(operand[0], weight_all[0:cols, at], preferred_element_type=F32)
            a = a + jnp.dot(operand[1], weight_all[cols:, at], preferred_element_type=F32)
            b = jnp.tanh(a[0:tokens])
            slope = 1.0 - b * b
            act[c, rows(0), at] = b
            out[c, rows(0), at] = (whole[c, core, rows(0), at].astype(F32) + b).astype(BF16)
            for k in range(1, dirs + 1):
                bk = slope * a[k * tokens : (k + 1) * tokens]
                act[c, rows(k), at] = bk
                out[c, rows(k), at] = (whole[c, core, rows(k), at].astype(F32) + bk).astype(BF16)
            return carry

        lax.fori_loop(0, tiles, product, 0)

        @pl.when(pos < last)
        def _():
            hop(c).start()

    def backward(c):
        @pl.when(pos == last)
        def _():
            error = out[c, rows(0), :].astype(F32) - target_ref[c].astype(F32)
            cot_in[c, rows(0), :] = error.astype(BF16)
            cot_in[c, tokens:, :] = out[c, tokens:, :]

        @pl.when(pos < last)
        def _():
            back(c).wait_recv()

        for j in range(tiles):
            at = pl.ds(j * tile, tile)
            c0 = cot_in[c, rows(0), at].astype(F32)
            b = act[c, rows(0), at]
            slope = 1.0 - b * b
            twice = 2.0 * b * c0
            gstack[rows(0), at] = (c0 * slope).astype(BF16)
            for k in range(1, dirs + 1):
                ck = cot_in[c, rows(k), at].astype(F32)
                gstack[rows(k), at] = (ck * slope - twice * act[c, rows(k), at]).astype(BF16)

        s = stats[c, 0, :, 0:1]
        u = [stats[c, k + 1, :, 0:1] for k in range(dirs)]

        def product(j, sums):
            half = j // tiles
            at = pl.ds(pl.multiple_of((j % tiles) * tile, tile), tile)
            q_all = lax.dot_general(
                gstack[...],
                weight_all[pl.ds(pl.multiple_of(j * tile, tile), tile), :],
                (((1,), (1,)), ((), ())),
                preferred_element_type=F32,
            )
            q[half, :, at] = q_all
            h = whole[c, half, rows(0), at].astype(F32)
            gain = gain_ref[half, :, at]
            q0 = q_all[0:tokens]
            n = h * s
            p = q0 * gain
            new = [sums[0] + fold(p * h)]
            for k in range(dirs):
                t = whole[c, half, rows(k + 1), at].astype(F32)
                qk = q_all[(k + 1) * tokens : (k + 2) * tokens]
                v = t * s + h * u[k]
                pk = qk * gain + q0 * probe_at(half, k, at)
                new.append(sums[k + 1] + fold(pk * h + p * t))
                acc_ref[half, k : k + 1, at] += jnp.sum(qk * n + q0 * v, axis=0, keepdims=True)
            return tuple(new)

        zero = jnp.zeros((tokens, 128), F32)
        sums = lax.fori_loop(0, 2 * tiles, product, (zero,) * (dirs + 1))

        @pl.when(pos > 0)
        def _():
            w = [jnp.sum(value, axis=-1, keepdims=True) for value in sums]
            cube = s * s * s / features
            w0 = cube * w[0]
            pull = [(3.0 / features) * s * s * u[k] * w[0] + cube * w[k + 1] for k in range(dirs)]

            def leaving(half, at):
                h = whole[c, half, rows(0), at].astype(F32)
                gain = gain_ref[half, :, at]
                q0 = q[half, rows(0), at]
                p = q0 * gain
                yield s * p - h * w0
                for k in range(dirs):
                    t = whole[c, half, rows(k + 1), at].astype(F32)
                    pk = q[half, rows(k + 1), at] * gain + q0 * probe_at(half, k, at)
                    yield u[k] * p + s * pk - h * pull[k] - t * w0

            for j in range(tiles):
                at = pl.ds(j * tile, tile)
                for k, value in enumerate(leaving(1 - core, at)):
                    part_out[c, rows(k), at] = value.astype(BF16)
            exchange = part(c)
            exchange.start()
            for j in range(tiles):
                at = pl.ds(j * tile, tile)
                for k, value in enumerate(list(leaving(core, at))):
                    q[core, rows(k), at] = value + cot_in[c, rows(k), at].astype(F32)
            exchange.wait_recv()
            for j in range(tiles):
                at = pl.ds(j * tile, tile)
                cot_out[c, :, at] = (q[core, :, at] + part_in[c, :, at].astype(F32)).astype(BF16)
            back(c).start()

    lag = jnp.minimum(lag_step * (last - pos), chunks)

    def turn(i, carry):
        @pl.when(i < chunks)
        def _():
            forward(jnp.minimum(i, chunks - 1))

        @pl.when((i >= lag) & (i - lag < chunks))
        def _():
            backward(jnp.clip(i - lag, 0, chunks - 1))

        return carry

    lax.fori_loop(0, chunks + min(lag_step * last, chunks), turn, 0)

    def drain(c, carry):
        @pl.when(pos < last)
        def _():
            hop(c).wait_send()

        @pl.when(pos > 0)
        def _():
            sibling(c).wait_send()
            part(c).wait_send()
            back(c).wait_send()

        return carry

    lax.fori_loop(0, chunks, drain, 0)

    drain_gather()


def settle_kernel(scale, divisor, crossed, parts_ref, probe_ref, hvp_ref, next_ref, got, tiles, sends, recvs, tile_sends, tile_recvs):
    owners, dirs, width = parts_ref.shape
    sections = lax.axis_size("section")
    dp, pos, core = lax.axis_index("dp"), lax.axis_index("section"), lax.axis_index("mp")
    pairs = [(i, j) for i in range(dirs) for j in range(i + 1)]
    group = 2 * owners
    everyone = owners * sections
    me = dp * 2 + core
    place = dp * sections + pos

    barrier = pltpu.get_barrier_semaphore()

    def greet_owner(step, carry):
        peer = lax.rem(me + step, group)
        target = {"dp": peer // 2, "mp": lax.rem(peer, 2)}
        pl.semaphore_signal(barrier, inc=1, device_id=target, device_id_type=MESH)
        return carry

    def greet_other(step, carry):
        target = {"dp": lax.rem(step, owners), "section": lax.rem(pos + 1 + step // owners, sections)}
        pl.semaphore_signal(barrier, inc=1, device_id=target, device_id_type=MESH)
        return carry

    def greet_all(step, carry):
        peer = lax.rem(place * 2 + core + step, 2 * everyone)
        spot = peer // 2
        target = {"dp": spot // sections, "section": lax.rem(spot, sections), "mp": lax.rem(peer, 2)}
        pl.semaphore_signal(barrier, inc=1, device_id=target, device_id_type=MESH)
        return carry

    if crossed:
        lax.fori_loop(1, 2 * everyone, greet_all, 0)
        pl.semaphore_wait(barrier, 2 * everyone - 1)
    else:
        lax.fori_loop(1, group, greet_owner, 0)
        lax.fori_loop(0, owners * (sections - 1), greet_other, 0)
        pl.semaphore_wait(barrier, group - 1 + owners * (sections - 1))

    def give(step):
        peer = lax.rem(me + step, group)
        return pltpu.make_async_remote_copy(
            src_ref=parts_ref.at[peer // 2],
            dst_ref=got.at[step],
            send_sem=sends.at[step],
            recv_sem=recvs.at[step],
            device_id={"dp": peer // 2, "mp": lax.rem(peer, 2)},
            device_id_type=MESH,
        )

    def start_give(step, carry):
        give(step).start()
        return carry

    def take(step, total):
        give(step).wait_recv()
        return total + got[step]

    def cross(slot):
        spot = pos * 2 + core
        return pltpu.make_async_remote_copy(
            src_ref=parts_ref.at[slot // 2],
            dst_ref=got.at[spot],
            send_sem=sends.at[slot],
            recv_sem=recvs.at[spot],
            device_id={"dp": slot // 2, "section": dp, "mp": lax.rem(slot, 2)},
            device_id_type=MESH,
        )

    def cross_in(slot):
        return pltpu.make_async_remote_copy(
            src_ref=got.at[slot],
            dst_ref=got.at[slot],
            send_sem=sends.at[slot],
            recv_sem=recvs.at[slot],
            device_id={"dp": pos, "section": slot // 2, "mp": lax.rem(slot, 2)},
            device_id_type=MESH,
        )

    def away(slot):
        return ~((dp == pos) & (slot == pos * 2 + core))

    if crossed:
        for slot in range(group):

            @pl.when(away(slot))
            def _():
                cross(slot).start()

        @pl.when(dp == pos)
        def _():
            got[pos * 2 + core] = parts_ref[dp]

        total = jnp.zeros(probe_ref.shape, F32)
        for slot in range(group):

            @pl.when(away(slot))
            def _():
                cross_in(slot).wait_recv()

            total = total + got[slot]
        curvature = total / divisor
    else:
        lax.fori_loop(1, group, start_give, 0)
        curvature = lax.fori_loop(1, group, take, parts_ref[dp]) / divisor
    hvp_ref[...] = curvature
    moved = probe_ref[...] + ETA * curvature
    row = lax.broadcasted_iota(jnp.int32, (16, 128), 0)
    tile = jnp.zeros((16, 128), F32)
    for index, (i, j) in enumerate(pairs):
        inner = jnp.sum(moved[i : i + 1] * moved[j : j + 1], axis=1, keepdims=True)
        tile = jnp.where(row == index, inner, tile)
    tiles[0] = tile

    def tell(step):
        peer = lax.rem(place + step, everyone)
        return pltpu.make_async_remote_copy(
            src_ref=tiles.at[0],
            dst_ref=tiles.at[step],
            send_sem=tile_sends.at[step],
            recv_sem=tile_recvs.at[step],
            device_id={"dp": peer // sections, "section": lax.rem(peer, sections)},
            device_id_type=MESH,
        )

    def start_tell(step, carry):
        tell(step).start()
        return carry

    lax.fori_loop(1, everyone, start_tell, 0)

    def hear(step, carry):
        tell(step).wait_recv()
        return carry

    lax.fori_loop(1, everyone, hear, 0)
    gram = lax.fori_loop(
        0,
        everyone,
        lambda source, total: total + tiles[lax.rem(place - source + everyone, everyone)],
        jnp.zeros((16, 128), F32),
    )
    entry = {pair: gram[index : index + 1, 0:1] for index, pair in enumerate(pairs)}
    factor = {}
    for j in range(dirs):
        rest = entry[j, j]
        for k in range(j):
            rest = rest - factor[j, k] * factor[j, k]
        factor[j, j] = jnp.sqrt(rest)
        for i in range(j + 1, dirs):
            rest = entry[i, j]
            for k in range(j):
                rest = rest - factor[i, k] * factor[j, k]
            factor[i, j] = rest / factor[j, j]
    solved = []
    for i in range(dirs):
        value = moved[i : i + 1]
        for k in range(i):
            value = value - factor[i, k] * solved[k]
        solved.append(value / factor[i, i])
        next_ref[i : i + 1, :] = solved[i] * scale

    def drain_give(step, carry):
        give(step).wait_send()
        return carry

    def drain_tell(step, carry):
        tell(step).wait_send()
        return carry

    if crossed:
        for slot in range(group):

            @pl.when(away(slot))
            def _():
                cross(slot).wait_send()

    else:
        lax.fori_loop(1, group, drain_give, 0)
    lax.fori_loop(1, everyone, drain_tell, 0)


def settle(accumulated, own_probe, scale, divisor, crossed):
    dirs, width = own_probe.shape
    owners, sections = lax.axis_size("dp"), lax.axis_size("section")
    vmem = pl.BlockSpec(memory_space=pltpu.VMEM)
    return pl.pallas_call(
        functools.partial(settle_kernel, scale, divisor, crossed),
        out_shape=[jax.ShapeDtypeStruct((dirs, width), F32)] * 2,
        in_specs=[vmem] * 2,
        out_specs=[vmem] * 2,
        scratch_shapes=[
            pltpu.VMEM((2 * owners, dirs, width), F32),
            pltpu.VMEM((owners * sections, 16, 128), F32),
        ]
        + [pltpu.SemaphoreType.DMA((2 * owners,))] * 2
        + [pltpu.SemaphoreType.DMA((owners * sections,))] * 2,
        compiler_params=pltpu.CompilerParams(
            collective_id=1, has_side_effects=True, vmem_limit_bytes=16 * 1024 * 1024
        ),
    )(accumulated.reshape(dirs, owners, width).transpose(1, 0, 2), own_probe)


def relay(inputs, target, gain, probe, weight, sections, chunk_tokens, lag_step, crossed):
    features = inputs.shape[-1]
    cols = features // 2
    dirs = probe.shape[0]
    chunks = inputs.shape[0] * inputs.shape[1] // chunk_tokens
    height = (dirs + 1) * chunk_tokens
    vmem = pl.BlockSpec(memory_space=pltpu.VMEM)
    dma = pltpu.SemaphoreType.DMA((chunks,))
    ring = pltpu.SemaphoreType.DMA((lax.axis_size("dp"),))
    extra = []
    if crossed:
        extra = [
            pltpu.VMEM((chunks, chunk_tokens, features), BF16),
            pltpu.VMEM((chunks, chunk_tokens, cols), BF16),
            pltpu.VMEM((2, 1, cols), F32),
            pltpu.VMEM((sections, weight.shape[0] // sections, cols), BF16),
            pltpu.SemaphoreType.DMA((15, sections)),
            pltpu.SemaphoreType.DMA((2,)),
            pltpu.SemaphoreType.DMA((5,)),
        ]
    acc = pl.pallas_call(
        functools.partial(relay_kernel, sections, lag_step, crossed),
        out_shape=jax.ShapeDtypeStruct((2, dirs, cols), F32),
        in_specs=[vmem] * 4 + [pl.BlockSpec(memory_space=pl.ANY)],
        out_specs=vmem,
        scratch_shapes=[
            pltpu.VMEM((features, cols), BF16),
            pltpu.VMEM((dirs, features), F32),
            pltpu.VMEM((chunks, 2, height, cols), BF16),
            pltpu.VMEM((chunks, height, cols), F32),
            pltpu.VMEM((chunks, height, cols), BF16),
            pltpu.VMEM((chunks, height, cols), BF16),
            pltpu.VMEM((chunks, height, cols), BF16),
            pltpu.VMEM((chunks, height, cols), BF16),
            pltpu.VMEM((chunks, height, cols), BF16),
            pltpu.VMEM((2, height, cols), BF16),
            pltpu.VMEM((height, cols), BF16),
            pltpu.VMEM((2, height, cols), F32),
            pltpu.VMEM((chunks, dirs + 1, chunk_tokens, 128), F32),
        ]
        + [dma] * 8
        + [ring] * 6
        + [pltpu.SemaphoreType.DMA]
        + extra,
        compiler_params=pltpu.CompilerParams(
            collective_id=0, has_side_effects=True, vmem_limit_bytes=56 * 1024 * 1024
        ),
        cost_estimate=pl.CostEstimate(
            flops=4 * chunks * height * features * cols, bytes_accessed=2 * features * cols, transcendentals=0
        ),
    )(
        inputs.reshape(chunks, chunk_tokens, features),
        target.reshape(chunks, chunk_tokens, cols),
        gain.reshape(2, 1, cols),
        probe,
        weight,
    )
    return acc.transpose(1, 0, 2).reshape(dirs, features)


def local(inputs, target, gains, weights, probes):
    sections = lax.axis_size("section")
    batches, micro_batch_tokens, features = inputs.shape
    probe_block = probes[:, 0, :]
    crossed = lax.axis_size("dp") == sections == 4 and probe_block.shape[1] % 128 == 0 and weights.shape[1] % 128 == 0
    if probe_block.shape[1] % 128:
        probe_block = lax.all_gather(probe_block, "dp", axis=1, tiled=True)
    accumulated = relay(inputs, target, gains[0], probe_block, weights[0], sections, 16, 3, crossed)
    divisor = batches * micro_batch_tokens * lax.axis_size("dp")
    curvature, rotated = settle(accumulated, probes[:, 0, :], math.sqrt(sections * features), divisor, crossed)
    return (curvature[:, None, :], rotated[:, None, :])


def solution(mesh):
    in_specs = (
        P(None, "dp", None),
        P(None, "dp", "mp"),
        P("section", None),
        P("section", "dp", "mp"),
        P(None, "section", "dp"),
    )
    out_specs = (P(None, "section", "dp"), P(None, "section", "dp"))
    return jax.shard_map(local, mesh=mesh, in_specs=in_specs, out_specs=out_specs, check_vma=False)
```

```python
import functools
import math

import jax
import jax.numpy as jnp
from jax import lax
from jax.experimental import pallas as pl
from jax.experimental.pallas import tpu as pltpu
from jax.sharding import PartitionSpec as P

EPS = 1e-05
ETA = 0.5
MESH = pl.DeviceIdType.MESH
F32 = jnp.float32
BF16 = jnp.bfloat16


def fold(values):
    total = values[..., 0:128]
    for start in range(128, values.shape[-1], 128):
        total = total + values[..., start : start + 128]
    return total


def straight_gather(pos, last, core, weight_block_ref, weight_all, probe_block_ref, probe_all, right_send, right_recv, left_send, left_recv, probe_send, probe_recv, own_sem):
    owners = lax.axis_size("dp")
    me = lax.axis_index("dp")
    depth = weight_block_ref.shape[0]
    width = probe_block_ref.shape[1]
    gather_probes = width < probe_all.shape[1]

    barrier = pltpu.get_barrier_semaphore()
    pl.semaphore_signal(barrier, inc=1, device_id={"mp": 1 - core}, device_id_type=MESH)

    @pl.when(pos > 0)
    def _():
        pl.semaphore_signal(barrier, inc=1, device_id={"section": pos - 1}, device_id_type=MESH)

    @pl.when(pos < last)
    def _():
        pl.semaphore_signal(barrier, inc=1, device_id={"section": pos + 1}, device_id_type=MESH)

    def block_rows(b):
        return pl.ds(pl.multiple_of(b * depth, depth), depth)

    def greet(step, carry):
        peer = lax.rem(me + step, owners)
        pl.semaphore_signal(barrier, inc=1, device_id={"dp": peer}, device_id_type=MESH)
        return carry

    lax.fori_loop(1, owners, greet, 0)
    own = pltpu.make_async_copy(weight_block_ref, weight_all.at[block_rows(me)], own_sem)
    own.start()
    peers = owners + (pos > 0).astype(jnp.int32) + (pos < last).astype(jnp.int32)
    pl.semaphore_wait(barrier, peers)
    own.wait()

    def to_right(b):
        return pltpu.make_async_remote_copy(
            src_ref=weight_all.at[block_rows(b)],
            dst_ref=weight_all.at[block_rows(b)],
            send_sem=right_send.at[b],
            recv_sem=right_recv.at[b],
            device_id={"dp": me + 1},
            device_id_type=MESH,
        )

    def to_left(b):
        return pltpu.make_async_remote_copy(
            src_ref=weight_all.at[block_rows(b)],
            dst_ref=weight_all.at[block_rows(b)],
            send_sem=left_send.at[b],
            recv_sem=left_recv.at[b],
            device_id={"dp": me - 1},
            device_id_type=MESH,
        )

    @pl.when(me < owners - 1)
    def _():
        to_right(me).start()

    @pl.when(me > 0)
    def _():
        to_left(me).start()

    def probe_to(step):
        mine = pl.ds(pl.multiple_of(me * width, width), width)
        return pltpu.make_async_remote_copy(
            src_ref=probe_all.at[:, mine],
            dst_ref=probe_all.at[:, mine],
            send_sem=probe_send.at[step],
            recv_sem=probe_recv.at[step],
            device_id={"dp": lax.rem(me + step, owners)},
            device_id_type=MESH,
        )

    if gather_probes:
        probe_all[:, pl.ds(pl.multiple_of(me * width, width), width)] = probe_block_ref[...]

        def spread(step, carry):
            probe_to(step).start()
            return carry

        lax.fori_loop(1, owners, spread, 0)
    else:
        probe_all[...] = probe_block_ref[...]


    def relay_blocks(step, carry):
        low, high = me - step, me + step

        @pl.when(low >= 0)
        def _():
            to_right(low).wait_recv()

            @pl.when(me < owners - 1)
            def _():
                to_right(low).start()

        @pl.when(high < owners)
        def _():
            to_left(high).wait_recv()

            @pl.when(me > 0)
            def _():
                to_left(high).start()

        return carry

    lax.fori_loop(1, owners, relay_blocks, 0)
    if gather_probes:

        def probes_in(step, carry):
            probe_to(step).wait_recv()
            return carry

        lax.fori_loop(1, owners, probes_in, 0)


    def drain():
        def drain_blocks(b, carry):
            @pl.when((me < owners - 1) & (b <= me))
            def _():
                to_right(b).wait_send()

            @pl.when((me > 0) & (b >= me))
            def _():
                to_left(b).wait_send()

            return carry

        lax.fori_loop(0, owners, drain_blocks, 0)
        if gather_probes:

            def drain_probes(step, carry):
                probe_to(step).wait_send()
                return carry

            lax.fori_loop(1, owners, drain_probes, 0)

    return drain


def crossed_gather(
    inputs_arg, target_arg, gain_arg, probe_block_ref, weight_block_ref, weight_all, probe_all,
    inputs_buf, target_buf, gain_buf, stage, sems, local_sems, one_sems,
):
    owners = lax.axis_size("dp")
    plane, column, core = lax.axis_index("dp"), lax.axis_index("section"), lax.axis_index("mp")
    depth = weight_block_ref.shape[0]
    piece = depth // owners
    width = probe_block_ref.shape[1]
    place = plane * owners + column
    out_send, out_recv, up_send, up_recv, x_send, x_recv, y_send, y_recv = [sems.at[i] for i in range(8)]
    fx_send, fx_recv, fy_send, fy_recv, probe_send, probe_recv, gain_send = [sems.at[i] for i in range(8, 15)]

    def flip(value, bits):
        for bit in (1, 2):
            if bits & bit:
                value = value + bit - 2 * bit * (value // bit % 2)
        return value

    barrier = pltpu.get_barrier_semaphore()

    def greet(step, carry):
        peer = lax.rem(place + step, owners * owners)
        target = {"dp": peer // owners, "section": lax.rem(peer, owners)}
        pl.semaphore_signal(barrier, inc=1, device_id=target, device_id_type=MESH)
        return carry

    lax.fori_loop(1, owners * owners, greet, 0)
    pl.semaphore_signal(barrier, inc=1, device_id={"mp": 1 - core}, device_id_type=MESH)
    pl.semaphore_wait(barrier, owners * owners)

    def remote(src, dst, send, recv, **target):
        return pltpu.make_async_remote_copy(
            src_ref=src, dst_ref=dst, send_sem=send, recv_sem=recv, device_id=target, device_id_type=MESH
        )

    def rows_of(k, t, start=0, count=piece):
        return weight_all.at[pl.ds(pl.multiple_of(k * depth + t * piece + start, 16), count)]

    def out(t):
        src = weight_block_ref.at[pl.ds(pl.multiple_of(t * piece, 16), piece)]
        return remote(src, stage.at[column], out_send.at[t], out_recv.at[column], section=t)

    def out_in(s):
        return remote(stage.at[s], stage.at[s], out_send.at[s], out_recv.at[s], section=s)

    def up(r):
        return remote(stage.at[r], rows_of(plane, column), up_send.at[r], up_recv.at[plane], dp=r)

    def up_in(k):
        return remote(stage.at[k], rows_of(k, column), up_send.at[k], up_recv.at[k], dp=k)

    half = piece // 2
    near_x, near_y, far = flip(column, 1), flip(column, 2), flip(column, 3)

    def to_x(k, t):
        return remote(rows_of(k, t), rows_of(k, t), x_send.at[k], x_recv.at[k], section=near_x)

    def to_y(k, t):
        return remote(rows_of(k, t), rows_of(k, t), y_send.at[k], y_recv.at[k], section=near_y)

    def on_x(k, t):
        rows = rows_of(k, t, half, half)
        return remote(rows, rows, fx_send.at[k], fx_recv.at[k], section=near_x)

    def on_y(k, t):
        rows = rows_of(k, t, 0, half)
        return remote(rows, rows, fy_send.at[k], fy_recv.at[k], section=near_y)

    first_stage = pltpu.make_async_copy(
        weight_block_ref.at[pl.ds(pl.multiple_of(column * piece, 16), piece)], stage.at[column], local_sems.at[0]
    )
    keep = pltpu.make_async_copy(stage.at[plane], rows_of(plane, column), local_sems.at[1])
    for bits in (3, 1, 2):
        out(flip(column, bits)).start()
    first_stage.start()

    def give_probe(t):
        mine = probe_all.at[:, pl.ds(pl.multiple_of(plane * width, 128), width)]
        return remote(probe_block_ref, mine, probe_send.at[t], probe_recv.at[plane], dp=column, section=t)

    def take_probe(k):
        mine = probe_all.at[:, pl.ds(pl.multiple_of(k * width, 128), width)]
        return remote(probe_block_ref, mine, probe_send.at[k], probe_recv.at[k], dp=k, section=plane)

    def give_gain(t):
        return remote(gain_arg, gain_buf, gain_send.at[t], one_sems.at[0], section=t)

    give_inputs = remote(inputs_arg, inputs_buf, one_sems.at[1], one_sems.at[2], dp=0)
    give_target = remote(target_arg, target_buf, one_sems.at[3], one_sems.at[4], dp=owners - 1)
    diagonal = plane == column
    for t in range(owners):

        @pl.when(~(diagonal & (column == t)))
        def _():
            give_probe(t).start()

        @pl.when(diagonal & (column != t))
        def _():
            give_gain(t).start()

    @pl.when(diagonal)
    def _():
        probe_all[:, pl.ds(pl.multiple_of(plane * width, 128), width)] = probe_block_ref[...]
        gain_buf[...] = gain_arg[...]

    @pl.when(diagonal & (plane != 0))
    def _():
        give_inputs.start()

    @pl.when(diagonal & (plane == 0))
    def _():
        inputs_buf[...] = inputs_arg[...]

    @pl.when(diagonal & (plane != owners - 1))
    def _():
        give_target.start()

    @pl.when(diagonal & (plane == owners - 1))
    def _():
        target_buf[...] = target_arg[...]

    first_stage.wait()
    for bits in (1, 2, 3):
        out_in(flip(column, bits)).wait_recv()
    keep.start()

    def pass_on(k):
        to_x(k, near_x).wait_recv()
        on_y(k, near_x).start()
        to_y(k, near_y).wait_recv()
        on_x(k, near_y).start()

    steps = [0]
    for d in range(1, owners):
        steps += [d, -d]

    def when_valid(d, body):
        k = plane + d

        @pl.when((k >= 0) & (k < owners))
        def _():
            body(k)

    def launch(k):
        to_x(k, column).start()
        to_y(k, column).start()

    def send_up(k):
        up(k).start()

    def sent_up(k):
        up(k).wait_send()

    for index, d in enumerate(steps):
        if d >= 0:
            for sign in (1, -1):
                if d > 0:
                    when_valid(sign * d, sent_up)
                if d + 1 < owners:
                    when_valid(sign * (d + 1), send_up)
        if d == 0:
            keep.wait()
            launch(plane)
        else:

            def arrive(k):
                up_in(k).wait_recv()
                launch(k)

            when_valid(d, arrive)
        if index > 0:
            when_valid(steps[index - 1], pass_on)
    when_valid(steps[-1], pass_on)
    for k in range(owners):
        on_x(k, far).wait_recv()
        on_y(k, far).wait_recv()

        @pl.when(~(diagonal & (plane == k)))
        def _():
            take_probe(k).wait_recv()

    @pl.when(~diagonal)
    def _():
        give_gain(column).wait_recv()

    @pl.when((plane == 0) & (column != 0))
    def _():
        give_inputs.wait_recv()

    @pl.when((plane == owners - 1) & (column != owners - 1))
    def _():
        give_target.wait_recv()

    def drain():
        for k in range(owners):
            to_x(k, column).wait_send()
            to_y(k, column).wait_send()
            on_x(k, near_y).wait_send()
            on_y(k, near_x).wait_send()

            @pl.when(column != k)
            def _():
                out(k).wait_send()

            @pl.when(~(diagonal & (column == k)))
            def _():
                give_probe(k).wait_send()

            @pl.when(diagonal & (column != k))
            def _():
                give_gain(k).wait_send()

        @pl.when(diagonal & (plane != 0))
        def _():
            give_inputs.wait_send()

        @pl.when(diagonal & (plane != owners - 1))
        def _():
            give_target.wait_send()

    return drain


def relay_kernel(
    sections,
    lag_step,
    crossed,
    inputs_arg,
    target_arg,
    gain_arg,
    probe_block_ref,
    weight_block_ref,
    acc_ref,
    weight_all,
    probe_all,
    whole,
    act,
    out,
    cot_in,
    cot_out,
    part_out,
    part_in,
    operand,
    gstack,
    q,
    stats,
    hop_send,
    hop_recv,
    sib_send,
    sib_recv,
    part_send,
    part_recv,
    back_send,
    back_recv,
    right_send,
    right_recv,
    left_send,
    left_recv,
    probe_send,
    probe_recv,
    own_sem,
    *crossed_scratch,
):
    pipe = "dp" if crossed else "section"
    pos = lax.axis_index(pipe)
    core = lax.axis_index("mp")
    last = sections - 1
    chunks, tokens, features = inputs_arg.shape
    if crossed:
        inputs_ref, target_ref, gain_ref = crossed_scratch[:3]
    else:
        inputs_ref, target_ref, gain_ref = inputs_arg, target_arg, gain_arg
    cols = features // 2
    dirs = probe_all.shape[0]
    tile = 512 if cols % 512 == 0 else 256 if cols % 256 == 0 else 128
    tiles = cols // tile

    def hop(c):
        return pltpu.make_async_remote_copy(
            src_ref=out.at[c],
            dst_ref=whole.at[c, core],
            send_sem=hop_send.at[c],
            recv_sem=hop_recv.at[c],
            device_id={pipe: pos + 1},
            device_id_type=MESH,
        )

    def sibling(c):
        return pltpu.make_async_remote_copy(
            src_ref=whole.at[c, core],
            dst_ref=whole.at[c, core],
            send_sem=sib_send.at[c],
            recv_sem=sib_recv.at[c],
            device_id={"mp": 1 - core},
            device_id_type=MESH,
        )

    def part(c):
        return pltpu.make_async_remote_copy(
            src_ref=part_out.at[c],
            dst_ref=part_in.at[c],
            send_sem=part_send.at[c],
            recv_sem=part_recv.at[c],
            device_id={"mp": 1 - core},
            device_id_type=MESH,
        )

    def back(c):
        return pltpu.make_async_remote_copy(
            src_ref=cot_out.at[c],
            dst_ref=cot_in.at[c],
            send_sem=back_send.at[c],
            recv_sem=back_recv.at[c],
            device_id={pipe: pos - 1},
            device_id_type=MESH,
        )

    def probe_at(half, k, at):
        start = half * cols + at.start
        if not isinstance(start, int):
            start = pl.multiple_of(start, 128)
        return probe_all[k : k + 1, pl.ds(start, tile)]

    def rows(k):
        return pl.ds(k * tokens, tokens)

    acc_ref[...] = jnp.zeros_like(acc_ref)

    if crossed:
        drain_gather = crossed_gather(
            inputs_arg, target_arg, gain_arg, probe_block_ref, weight_block_ref, weight_all, probe_all, *crossed_scratch
        )
    else:
        drain_gather = straight_gather(
            pos, last, core, weight_block_ref, weight_all, probe_block_ref, probe_all,
            right_send, right_recv, left_send, left_recv, probe_send, probe_recv, own_sem,
        )

    def forward(c):
        @pl.when(pos == 0)
        def _():
            for half in range(2):
                whole[c, half, 0:tokens, :] = inputs_ref[c, :, half * cols : (half + 1) * cols]
                whole[c, half, tokens:, :] = jnp.zeros((dirs * tokens, cols), BF16)

        @pl.when(pos > 0)
        def _():
            hop(c).wait_recv()
            swap = sibling(c)
            swap.start()
            swap.wait_recv()

        square = jnp.zeros((tokens, 128), F32)
        cross = [jnp.zeros((tokens, 128), F32) for _ in range(dirs)]
        for half in range(2):
            for j in range(tiles):
                at = pl.ds(j * tile, tile)
                h = whole[c, half, rows(0), at].astype(F32)
                square = square + fold(h * h)
                for k in range(dirs):
                    cross[k] = cross[k] + fold(h * whole[c, half, rows(k + 1), at].astype(F32))
        s = lax.rsqrt(jnp.sum(square, axis=-1, keepdims=True) / features + EPS)
        cube = -(s * s * s) / features
        u = [cube * jnp.sum(cross[k], axis=-1, keepdims=True) for k in range(dirs)]
        stats[c, 0] = jnp.broadcast_to(s, (tokens, 128))
        for k in range(dirs):
            stats[c, k + 1] = jnp.broadcast_to(u[k], (tokens, 128))
        for half in range(2):
            for j in range(tiles):
                at = pl.ds(j * tile, tile)
                h = whole[c, half, rows(0), at].astype(F32)
                gain = gain_ref[half, :, at]
                n = h * s
                operand[half, rows(0), at] = (n * gain).astype(BF16)
                for k in range(dirs):
                    t = whole[c, half, rows(k + 1), at].astype(F32)
                    mixed = (t * s + h * u[k]) * gain + n * probe_at(half, k, at)
                    operand[half, rows(k + 1), at] = mixed.astype(BF16)

        for j in range(tiles):
            at = pl.ds(j * tile, tile)
            a = jnp.dot(operand[0], weight_all[0:cols, at], preferred_element_type=F32)
            a = a + jnp.dot(operand[1], weight_all[cols:, at], preferred_element_type=F32)
            b = jnp.tanh(a[0:tokens])
            slope = 1.0 - b * b
            act[c, rows(0), at] = b
            out[c, rows(0), at] = (whole[c, core, rows(0), at].astype(F32) + b).astype(BF16)
            for k in range(1, dirs + 1):
                bk = slope * a[k * tokens : (k + 1) * tokens]
                act[c, rows(k), at] = bk
                out[c, rows(k), at] = (whole[c, core, rows(k), at].astype(F32) + bk).astype(BF16)

        @pl.when(pos < last)
        def _():
            hop(c).start()

    def backward(c):
        @pl.when(pos == last)
        def _():
            error = out[c, rows(0), :].astype(F32) - target_ref[c].astype(F32)
            cot_in[c, rows(0), :] = error.astype(BF16)
            cot_in[c, tokens:, :] = out[c, tokens:, :]

        @pl.when(pos < last)
        def _():
            back(c).wait_recv()

        for j in range(tiles):
            at = pl.ds(j * tile, tile)
            c0 = cot_in[c, rows(0), at].astype(F32)
            b = act[c, rows(0), at]
            slope = 1.0 - b * b
            twice = 2.0 * b * c0
            gstack[rows(0), at] = (c0 * slope).astype(BF16)
            for k in range(1, dirs + 1):
                ck = cot_in[c, rows(k), at].astype(F32)
                gstack[rows(k), at] = (ck * slope - twice * act[c, rows(k), at]).astype(BF16)

        s = stats[c, 0, :, 0:1]
        u = [stats[c, k + 1, :, 0:1] for k in range(dirs)]

        def product(j, sums):
            half = j // tiles
            at = pl.ds((j % tiles) * tile, tile)
            q_all = lax.dot_general(
                gstack[...],
                weight_all[pl.ds(j * tile, tile), :],
                (((1,), (1,)), ((), ())),
                preferred_element_type=F32,
            )
            q[half, :, at] = q_all
            h = whole[c, half, rows(0), at].astype(F32)
            gain = gain_ref[half, :, at]
            q0 = q_all[0:tokens]
            n = h * s
            p = q0 * gain
            new = [sums[0] + fold(p * h)]
            for k in range(dirs):
                t = whole[c, half, rows(k + 1), at].astype(F32)
                qk = q_all[(k + 1) * tokens : (k + 2) * tokens]
                v = t * s + h * u[k]
                pk = qk * gain + q0 * probe_at(half, k, at)
                new.append(sums[k + 1] + fold(pk * h + p * t))
                acc_ref[half, k : k + 1, at] += jnp.sum(qk * n + q0 * v, axis=0, keepdims=True)
            return tuple(new)

        zero = jnp.zeros((tokens, 128), F32)
        sums = (zero,) * (dirs + 1)
        for j in range(2 * tiles):
            sums = product(j, sums)

        @pl.when(pos > 0)
        def _():
            w = [jnp.sum(value, axis=-1, keepdims=True) for value in sums]
            cube = s * s * s / features
            w0 = cube * w[0]
            pull = [(3.0 / features) * s * s * u[k] * w[0] + cube * w[k + 1] for k in range(dirs)]

            def leaving(half, at):
                h = whole[c, half, rows(0), at].astype(F32)
                gain = gain_ref[half, :, at]
                q0 = q[half, rows(0), at]
                p = q0 * gain
                yield s * p - h * w0
                for k in range(dirs):
                    t = whole[c, half, rows(k + 1), at].astype(F32)
                    pk = q[half, rows(k + 1), at] * gain + q0 * probe_at(half, k, at)
                    yield u[k] * p + s * pk - h * pull[k] - t * w0

            for j in range(tiles):
                at = pl.ds(j * tile, tile)
                for k, value in enumerate(leaving(1 - core, at)):
                    part_out[c, rows(k), at] = value.astype(BF16)
            exchange = part(c)
            exchange.start()
            for j in range(tiles):
                at = pl.ds(j * tile, tile)
                for k, value in enumerate(list(leaving(core, at))):
                    q[core, rows(k), at] = value + cot_in[c, rows(k), at].astype(F32)
            exchange.wait_recv()
            for j in range(tiles):
                at = pl.ds(j * tile, tile)
                cot_out[c, :, at] = (q[core, :, at] + part_in[c, :, at].astype(F32)).astype(BF16)
            back(c).start()

    lag = jnp.minimum(lag_step * (last - pos), chunks)

    def turn(i, carry):
        @pl.when(i < chunks)
        def _():
            forward(jnp.minimum(i, chunks - 1))

        @pl.when((i >= lag) & (i - lag < chunks))
        def _():
            backward(jnp.clip(i - lag, 0, chunks - 1))

        return carry

    lax.fori_loop(0, chunks + min(lag_step * last, chunks), turn, 0)

    def drain(c, carry):
        @pl.when(pos < last)
        def _():
            hop(c).wait_send()

        @pl.when(pos > 0)
        def _():
            sibling(c).wait_send()
            part(c).wait_send()
            back(c).wait_send()

        return carry

    lax.fori_loop(0, chunks, drain, 0)

    drain_gather()


def settle_kernel(scale, divisor, crossed, parts_ref, probe_ref, hvp_ref, next_ref, got, tiles, sends, recvs, tile_sends, tile_recvs):
    owners, dirs, width = parts_ref.shape
    sections = lax.axis_size("section")
    dp, pos, core = lax.axis_index("dp"), lax.axis_index("section"), lax.axis_index("mp")
    pairs = [(i, j) for i in range(dirs) for j in range(i + 1)]
    group = 2 * owners
    everyone = owners * sections
    me = dp * 2 + core
    place = dp * sections + pos

    barrier = pltpu.get_barrier_semaphore()

    def greet_owner(step, carry):
        peer = lax.rem(me + step, group)
        target = {"dp": peer // 2, "mp": lax.rem(peer, 2)}
        pl.semaphore_signal(barrier, inc=1, device_id=target, device_id_type=MESH)
        return carry

    def greet_other(step, carry):
        target = {"dp": lax.rem(step, owners), "section": lax.rem(pos + 1 + step // owners, sections)}
        pl.semaphore_signal(barrier, inc=1, device_id=target, device_id_type=MESH)
        return carry

    def greet_all(step, carry):
        peer = lax.rem(place * 2 + core + step, 2 * everyone)
        spot = peer // 2
        target = {"dp": spot // sections, "section": lax.rem(spot, sections), "mp": lax.rem(peer, 2)}
        pl.semaphore_signal(barrier, inc=1, device_id=target, device_id_type=MESH)
        return carry

    if crossed:
        lax.fori_loop(1, 2 * everyone, greet_all, 0)
        pl.semaphore_wait(barrier, 2 * everyone - 1)
    else:
        lax.fori_loop(1, group, greet_owner, 0)
        lax.fori_loop(0, owners * (sections - 1), greet_other, 0)
        pl.semaphore_wait(barrier, group - 1 + owners * (sections - 1))

    def give(step):
        peer = lax.rem(me + step, group)
        return pltpu.make_async_remote_copy(
            src_ref=parts_ref.at[peer // 2],
            dst_ref=got.at[step],
            send_sem=sends.at[step],
            recv_sem=recvs.at[step],
            device_id={"dp": peer // 2, "mp": lax.rem(peer, 2)},
            device_id_type=MESH,
        )

    def start_give(step, carry):
        give(step).start()
        return carry

    def take(step, total):
        give(step).wait_recv()
        return total + got[step]

    def cross(slot):
        spot = pos * 2 + core
        return pltpu.make_async_remote_copy(
            src_ref=parts_ref.at[slot // 2],
            dst_ref=got.at[spot],
            send_sem=sends.at[slot],
            recv_sem=recvs.at[spot],
            device_id={"dp": slot // 2, "section": dp, "mp": lax.rem(slot, 2)},
            device_id_type=MESH,
        )

    def cross_in(slot):
        return pltpu.make_async_remote_copy(
            src_ref=got.at[slot],
            dst_ref=got.at[slot],
            send_sem=sends.at[slot],
            recv_sem=recvs.at[slot],
            device_id={"dp": pos, "section": slot // 2, "mp": lax.rem(slot, 2)},
            device_id_type=MESH,
        )

    def away(slot):
        return ~((dp == pos) & (slot == pos * 2 + core))

    if crossed:
        for slot in range(group):

            @pl.when(away(slot))
            def _():
                cross(slot).start()

        @pl.when(dp == pos)
        def _():
            got[pos * 2 + core] = parts_ref[dp]

        total = jnp.zeros(probe_ref.shape, F32)
        for slot in range(group):

            @pl.when(away(slot))
            def _():
                cross_in(slot).wait_recv()

            total = total + got[slot]
        curvature = total / divisor
    else:
        lax.fori_loop(1, group, start_give, 0)
        curvature = lax.fori_loop(1, group, take, parts_ref[dp]) / divisor
    hvp_ref[...] = curvature
    moved = probe_ref[...] + ETA * curvature
    row = lax.broadcasted_iota(jnp.int32, (16, 128), 0)
    tile = jnp.zeros((16, 128), F32)
    for index, (i, j) in enumerate(pairs):
        inner = jnp.sum(moved[i : i + 1] * moved[j : j + 1], axis=1, keepdims=True)
        tile = jnp.where(row == index, inner, tile)
    tiles[0] = tile

    def tell(step):
        peer = lax.rem(place + step, everyone)
        return pltpu.make_async_remote_copy(
            src_ref=tiles.at[0],
            dst_ref=tiles.at[step],
            send_sem=tile_sends.at[step],
            recv_sem=tile_recvs.at[step],
            device_id={"dp": peer // sections, "section": lax.rem(peer, sections)},
            device_id_type=MESH,
        )

    def start_tell(step, carry):
        tell(step).start()
        return carry

    lax.fori_loop(1, everyone, start_tell, 0)

    def hear(step, carry):
        tell(step).wait_recv()
        return carry

    lax.fori_loop(1, everyone, hear, 0)
    gram = lax.fori_loop(
        0,
        everyone,
        lambda source, total: total + tiles[lax.rem(place - source + everyone, everyone)],
        jnp.zeros((16, 128), F32),
    )
    entry = {pair: gram[index : index + 1, 0:1] for index, pair in enumerate(pairs)}
    factor = {}
    for j in range(dirs):
        rest = entry[j, j]
        for k in range(j):
            rest = rest - factor[j, k] * factor[j, k]
        factor[j, j] = jnp.sqrt(rest)
        for i in range(j + 1, dirs):
            rest = entry[i, j]
            for k in range(j):
                rest = rest - factor[i, k] * factor[j, k]
            factor[i, j] = rest / factor[j, j]
    solved = []
    for i in range(dirs):
        value = moved[i : i + 1]
        for k in range(i):
            value = value - factor[i, k] * solved[k]
        solved.append(value / factor[i, i])
        next_ref[i : i + 1, :] = solved[i] * scale

    def drain_give(step, carry):
        give(step).wait_send()
        return carry

    def drain_tell(step, carry):
        tell(step).wait_send()
        return carry

    if crossed:
        for slot in range(group):

            @pl.when(away(slot))
            def _():
                cross(slot).wait_send()

    else:
        lax.fori_loop(1, group, drain_give, 0)
    lax.fori_loop(1, everyone, drain_tell, 0)


def settle(accumulated, own_probe, scale, divisor, crossed):
    dirs, width = own_probe.shape
    owners, sections = lax.axis_size("dp"), lax.axis_size("section")
    vmem = pl.BlockSpec(memory_space=pltpu.VMEM)
    return pl.pallas_call(
        functools.partial(settle_kernel, scale, divisor, crossed),
        out_shape=[jax.ShapeDtypeStruct((dirs, width), F32)] * 2,
        in_specs=[vmem] * 2,
        out_specs=[vmem] * 2,
        scratch_shapes=[
            pltpu.VMEM((2 * owners, dirs, width), F32),
            pltpu.VMEM((owners * sections, 16, 128), F32),
        ]
        + [pltpu.SemaphoreType.DMA((2 * owners,))] * 2
        + [pltpu.SemaphoreType.DMA((owners * sections,))] * 2,
        compiler_params=pltpu.CompilerParams(
            collective_id=1, has_side_effects=True, vmem_limit_bytes=16 * 1024 * 1024
        ),
    )(accumulated.reshape(dirs, owners, width).transpose(1, 0, 2), own_probe)


def relay(inputs, target, gain, probe, weight, sections, chunk_tokens, lag_step, crossed):
    features = inputs.shape[-1]
    cols = features // 2
    dirs = probe.shape[0]
    chunks = inputs.shape[0] * inputs.shape[1] // chunk_tokens
    height = (dirs + 1) * chunk_tokens
    vmem = pl.BlockSpec(memory_space=pltpu.VMEM)
    dma = pltpu.SemaphoreType.DMA((chunks,))
    ring = pltpu.SemaphoreType.DMA((lax.axis_size("dp"),))
    extra = []
    if crossed:
        extra = [
            pltpu.VMEM((chunks, chunk_tokens, features), BF16),
            pltpu.VMEM((chunks, chunk_tokens, cols), BF16),
            pltpu.VMEM((2, 1, cols), F32),
            pltpu.VMEM((sections, weight.shape[0] // sections, cols), BF16),
            pltpu.SemaphoreType.DMA((15, sections)),
            pltpu.SemaphoreType.DMA((2,)),
            pltpu.SemaphoreType.DMA((5,)),
        ]
    acc = pl.pallas_call(
        functools.partial(relay_kernel, sections, lag_step, crossed),
        out_shape=jax.ShapeDtypeStruct((2, dirs, cols), F32),
        in_specs=[vmem] * 4 + [pl.BlockSpec(memory_space=pl.ANY)],
        out_specs=vmem,
        scratch_shapes=[
            pltpu.VMEM((features, cols), BF16),
            pltpu.VMEM((dirs, features), F32),
            pltpu.VMEM((chunks, 2, height, cols), BF16),
            pltpu.VMEM((chunks, height, cols), F32),
            pltpu.VMEM((chunks, height, cols), BF16),
            pltpu.VMEM((chunks, height, cols), BF16),
            pltpu.VMEM((chunks, height, cols), BF16),
            pltpu.VMEM((chunks, height, cols), BF16),
            pltpu.VMEM((chunks, height, cols), BF16),
            pltpu.VMEM((2, height, cols), BF16),
            pltpu.VMEM((height, cols), BF16),
            pltpu.VMEM((2, height, cols), F32),
            pltpu.VMEM((chunks, dirs + 1, chunk_tokens, 128), F32),
        ]
        + [dma] * 8
        + [ring] * 6
        + [pltpu.SemaphoreType.DMA]
        + extra,
        compiler_params=pltpu.CompilerParams(
            collective_id=0, has_side_effects=True, vmem_limit_bytes=56 * 1024 * 1024
        ),
        cost_estimate=pl.CostEstimate(
            flops=4 * chunks * height * features * cols, bytes_accessed=2 * features * cols, transcendentals=0
        ),
    )(
        inputs.reshape(chunks, chunk_tokens, features),
        target.reshape(chunks, chunk_tokens, cols),
        gain.reshape(2, 1, cols),
        probe,
        weight,
    )
    return acc.transpose(1, 0, 2).reshape(dirs, features)


def local(inputs, target, gains, weights, probes):
    sections = lax.axis_size("section")
    batches, micro_batch_tokens, features = inputs.shape
    probe_block = probes[:, 0, :]
    crossed = lax.axis_size("dp") == sections == 4 and probe_block.shape[1] % 128 == 0 and weights.shape[1] % 128 == 0
    if probe_block.shape[1] % 128:
        probe_block = lax.all_gather(probe_block, "dp", axis=1, tiled=True)
    accumulated = relay(inputs, target, gains[0], probe_block, weights[0], sections, 16, 3, crossed)
    divisor = batches * micro_batch_tokens * lax.axis_size("dp")
    curvature, rotated = settle(accumulated, probes[:, 0, :], math.sqrt(sections * features), divisor, crossed)
    return (curvature[:, None, :], rotated[:, None, :])


def solution(mesh):
    in_specs = (
        P(None, "dp", None),
        P(None, "dp", "mp"),
        P("section", None),
        P("section", "dp", "mp"),
        P(None, "section", "dp"),
    )
    out_specs = (P(None, "section", "dp"), P(None, "section", "dp"))
    return jax.shard_map(local, mesh=mesh, in_specs=in_specs, out_specs=out_specs, check_vma=False)
```

```python
import functools
import math

import jax
import jax.numpy as jnp
from jax import lax
from jax.experimental import pallas as pl
from jax.experimental.pallas import tpu as pltpu
from jax.sharding import PartitionSpec as P

EPS = 1e-05
ETA = 0.5
MESH = pl.DeviceIdType.MESH
F32 = jnp.float32
BF16 = jnp.bfloat16


def fold(values):
    total = values[..., 0:128]
    for start in range(128, values.shape[-1], 128):
        total = total + values[..., start : start + 128]
    return total


def straight_gather(pos, last, core, weight_block_ref, weight_all, probe_block_ref, probe_all, right_send, right_recv, left_send, left_recv, probe_send, probe_recv, own_sem):
    owners = lax.axis_size("dp")
    me = lax.axis_index("dp")
    depth = weight_block_ref.shape[0]
    width = probe_block_ref.shape[1]
    gather_probes = width < probe_all.shape[1]

    barrier = pltpu.get_barrier_semaphore()
    pl.semaphore_signal(barrier, inc=1, device_id={"mp": 1 - core}, device_id_type=MESH)

    @pl.when(pos > 0)
    def _():
        pl.semaphore_signal(barrier, inc=1, device_id={"section": pos - 1}, device_id_type=MESH)

    @pl.when(pos < last)
    def _():
        pl.semaphore_signal(barrier, inc=1, device_id={"section": pos + 1}, device_id_type=MESH)

    def block_rows(b):
        return pl.ds(pl.multiple_of(b * depth, depth), depth)

    def greet(step, carry):
        peer = lax.rem(me + step, owners)
        pl.semaphore_signal(barrier, inc=1, device_id={"dp": peer}, device_id_type=MESH)
        return carry

    lax.fori_loop(1, owners, greet, 0)
    own = pltpu.make_async_copy(weight_block_ref, weight_all.at[block_rows(me)], own_sem)
    own.start()
    peers = owners + (pos > 0).astype(jnp.int32) + (pos < last).astype(jnp.int32)
    pl.semaphore_wait(barrier, peers)
    own.wait()

    def to_right(b):
        return pltpu.make_async_remote_copy(
            src_ref=weight_all.at[block_rows(b)],
            dst_ref=weight_all.at[block_rows(b)],
            send_sem=right_send.at[b],
            recv_sem=right_recv.at[b],
            device_id={"dp": me + 1},
            device_id_type=MESH,
        )

    def to_left(b):
        return pltpu.make_async_remote_copy(
            src_ref=weight_all.at[block_rows(b)],
            dst_ref=weight_all.at[block_rows(b)],
            send_sem=left_send.at[b],
            recv_sem=left_recv.at[b],
            device_id={"dp": me - 1},
            device_id_type=MESH,
        )

    @pl.when(me < owners - 1)
    def _():
        to_right(me).start()

    @pl.when(me > 0)
    def _():
        to_left(me).start()

    def probe_to(step):
        mine = pl.ds(pl.multiple_of(me * width, width), width)
        return pltpu.make_async_remote_copy(
            src_ref=probe_all.at[:, mine],
            dst_ref=probe_all.at[:, mine],
            send_sem=probe_send.at[step],
            recv_sem=probe_recv.at[step],
            device_id={"dp": lax.rem(me + step, owners)},
            device_id_type=MESH,
        )

    if gather_probes:
        probe_all[:, pl.ds(pl.multiple_of(me * width, width), width)] = probe_block_ref[...]

        def spread(step, carry):
            probe_to(step).start()
            return carry

        lax.fori_loop(1, owners, spread, 0)
    else:
        probe_all[...] = probe_block_ref[...]


    def relay_blocks(step, carry):
        low, high = me - step, me + step

        @pl.when(low >= 0)
        def _():
            to_right(low).wait_recv()

            @pl.when(me < owners - 1)
            def _():
                to_right(low).start()

        @pl.when(high < owners)
        def _():
            to_left(high).wait_recv()

            @pl.when(me > 0)
            def _():
                to_left(high).start()

        return carry

    lax.fori_loop(1, owners, relay_blocks, 0)
    if gather_probes:

        def probes_in(step, carry):
            probe_to(step).wait_recv()
            return carry

        lax.fori_loop(1, owners, probes_in, 0)


    def drain():
        def drain_blocks(b, carry):
            @pl.when((me < owners - 1) & (b <= me))
            def _():
                to_right(b).wait_send()

            @pl.when((me > 0) & (b >= me))
            def _():
                to_left(b).wait_send()

            return carry

        lax.fori_loop(0, owners, drain_blocks, 0)
        if gather_probes:

            def drain_probes(step, carry):
                probe_to(step).wait_send()
                return carry

            lax.fori_loop(1, owners, drain_probes, 0)

    return drain


def crossed_gather(
    inputs_arg, target_arg, gain_arg, probe_block_ref, weight_block_ref, weight_all, probe_all,
    inputs_buf, target_buf, gain_buf, stage, sems, local_sems, one_sems,
):
    owners = lax.axis_size("dp")
    plane, column, core = lax.axis_index("dp"), lax.axis_index("section"), lax.axis_index("mp")
    depth = weight_block_ref.shape[0]
    piece = depth // owners
    width = probe_block_ref.shape[1]
    place = plane * owners + column
    out_send, out_recv, up_send, up_recv, x_send, x_recv, y_send, y_recv = [sems.at[i] for i in range(8)]
    fx_send, fx_recv, fy_send, fy_recv, probe_send, probe_recv, gain_send = [sems.at[i] for i in range(8, 15)]

    def flip(value, bits):
        for bit in (1, 2):
            if bits & bit:
                value = value + bit - 2 * bit * (value // bit % 2)
        return value

    barrier = pltpu.get_barrier_semaphore()

    def greet(step, carry):
        peer = lax.rem(place + step, owners * owners)
        target = {"dp": peer // owners, "section": lax.rem(peer, owners)}
        pl.semaphore_signal(barrier, inc=1, device_id=target, device_id_type=MESH)
        return carry

    lax.fori_loop(1, owners * owners, greet, 0)
    pl.semaphore_signal(barrier, inc=1, device_id={"mp": 1 - core}, device_id_type=MESH)
    pl.semaphore_wait(barrier, owners * owners)

    def remote(src, dst, send, recv, **target):
        return pltpu.make_async_remote_copy(
            src_ref=src, dst_ref=dst, send_sem=send, recv_sem=recv, device_id=target, device_id_type=MESH
        )

    def rows_of(k, t, start=0, count=piece):
        return weight_all.at[pl.ds(pl.multiple_of(k * depth + t * piece + start, 16), count)]

    def out(t):
        src = weight_block_ref.at[pl.ds(pl.multiple_of(t * piece, 16), piece)]
        return remote(src, stage.at[column], out_send.at[t], out_recv.at[column], section=t)

    def out_in(s):
        return remote(stage.at[s], stage.at[s], out_send.at[s], out_recv.at[s], section=s)

    def up(r):
        return remote(stage.at[r], rows_of(plane, column), up_send.at[r], up_recv.at[plane], dp=r)

    def up_in(k):
        return remote(stage.at[k], rows_of(k, column), up_send.at[k], up_recv.at[k], dp=k)

    half = piece // 2
    near_x, near_y, far = flip(column, 1), flip(column, 2), flip(column, 3)

    def to_x(k, t):
        return remote(rows_of(k, t), rows_of(k, t), x_send.at[k], x_recv.at[k], section=near_x)

    def to_y(k, t):
        return remote(rows_of(k, t), rows_of(k, t), y_send.at[k], y_recv.at[k], section=near_y)

    def on_x(k, t):
        rows = rows_of(k, t, half, half)
        return remote(rows, rows, fx_send.at[k], fx_recv.at[k], section=near_x)

    def on_y(k, t):
        rows = rows_of(k, t, 0, half)
        return remote(rows, rows, fy_send.at[k], fy_recv.at[k], section=near_y)

    first_stage = pltpu.make_async_copy(
        weight_block_ref.at[pl.ds(pl.multiple_of(column * piece, 16), piece)], stage.at[column], local_sems.at[0]
    )
    keep = pltpu.make_async_copy(stage.at[plane], rows_of(plane, column), local_sems.at[1])
    for bits in (3, 1, 2):
        out(flip(column, bits)).start()
    first_stage.start()

    def give_probe(t):
        mine = probe_all.at[:, pl.ds(pl.multiple_of(plane * width, 128), width)]
        return remote(probe_block_ref, mine, probe_send.at[t], probe_recv.at[plane], dp=column, section=t)

    def take_probe(k):
        mine = probe_all.at[:, pl.ds(pl.multiple_of(k * width, 128), width)]
        return remote(probe_block_ref, mine, probe_send.at[k], probe_recv.at[k], dp=k, section=plane)

    def give_gain(t):
        return remote(gain_arg, gain_buf, gain_send.at[t], one_sems.at[0], section=t)

    give_inputs = remote(inputs_arg, inputs_buf, one_sems.at[1], one_sems.at[2], dp=0)
    give_target = remote(target_arg, target_buf, one_sems.at[3], one_sems.at[4], dp=owners - 1)
    diagonal = plane == column
    for t in range(owners):

        @pl.when(~(diagonal & (column == t)))
        def _():
            give_probe(t).start()

        @pl.when(diagonal & (column != t))
        def _():
            give_gain(t).start()

    @pl.when(diagonal)
    def _():
        probe_all[:, pl.ds(pl.multiple_of(plane * width, 128), width)] = probe_block_ref[...]
        gain_buf[...] = gain_arg[...]

    @pl.when(diagonal & (plane != 0))
    def _():
        give_inputs.start()

    @pl.when(diagonal & (plane == 0))
    def _():
        inputs_buf[...] = inputs_arg[...]

    @pl.when(diagonal & (plane != owners - 1))
    def _():
        give_target.start()

    @pl.when(diagonal & (plane == owners - 1))
    def _():
        target_buf[...] = target_arg[...]

    first_stage.wait()
    for bits in (1, 2, 3):
        out_in(flip(column, bits)).wait_recv()
    keep.start()

    def pass_on(k):
        to_x(k, near_x).wait_recv()
        on_y(k, near_x).start()
        to_y(k, near_y).wait_recv()
        on_x(k, near_y).start()

    steps = [0]
    for d in range(1, owners):
        steps += [d, -d]

    def when_valid(d, body):
        k = plane + d

        @pl.when((k >= 0) & (k < owners))
        def _():
            body(k)

    def launch(k):
        to_x(k, column).start()
        to_y(k, column).start()

    def send_up(k):
        up(k).start()

    def sent_up(k):
        up(k).wait_send()

    for index, d in enumerate(steps):
        if d >= 0:
            for sign in (1, -1):
                if d > 0:
                    when_valid(sign * d, sent_up)
                if d + 1 < owners:
                    when_valid(sign * (d + 1), send_up)
        if d == 0:
            keep.wait()
            launch(plane)
        else:

            def arrive(k):
                up_in(k).wait_recv()
                launch(k)

            when_valid(d, arrive)
        if index > 0:
            when_valid(steps[index - 1], pass_on)
    when_valid(steps[-1], pass_on)
    for k in range(owners):
        on_x(k, far).wait_recv()
        on_y(k, far).wait_recv()

        @pl.when(~(diagonal & (plane == k)))
        def _():
            take_probe(k).wait_recv()

    @pl.when(~diagonal)
    def _():
        give_gain(column).wait_recv()

    @pl.when((plane == 0) & (column != 0))
    def _():
        give_inputs.wait_recv()

    @pl.when((plane == owners - 1) & (column != owners - 1))
    def _():
        give_target.wait_recv()

    def drain():
        for k in range(owners):
            to_x(k, column).wait_send()
            to_y(k, column).wait_send()
            on_x(k, near_y).wait_send()
            on_y(k, near_x).wait_send()

            @pl.when(column != k)
            def _():
                out(k).wait_send()

            @pl.when(~(diagonal & (column == k)))
            def _():
                give_probe(k).wait_send()

            @pl.when(diagonal & (column != k))
            def _():
                give_gain(k).wait_send()

        @pl.when(diagonal & (plane != 0))
        def _():
            give_inputs.wait_send()

        @pl.when(diagonal & (plane != owners - 1))
        def _():
            give_target.wait_send()

    return drain


def relay_kernel(
    sections,
    lag_step,
    crossed,
    inputs_arg,
    target_arg,
    gain_arg,
    probe_block_ref,
    weight_block_ref,
    acc_ref,
    weight_all,
    probe_all,
    whole,
    act,
    out,
    cot_in,
    cot_out,
    part_out,
    part_in,
    operand,
    gstack,
    q,
    stats,
    hop_send,
    hop_recv,
    sib_send,
    sib_recv,
    part_send,
    part_recv,
    back_send,
    back_recv,
    right_send,
    right_recv,
    left_send,
    left_recv,
    probe_send,
    probe_recv,
    own_sem,
    *crossed_scratch,
):
    pipe = "dp" if crossed else "section"
    pos = lax.axis_index(pipe)
    core = lax.axis_index("mp")
    last = sections - 1
    chunks, tokens, features = inputs_arg.shape
    if crossed:
        inputs_ref, target_ref, gain_ref = crossed_scratch[:3]
    else:
        inputs_ref, target_ref, gain_ref = inputs_arg, target_arg, gain_arg
    cols = features // 2
    dirs = probe_all.shape[0]
    tile = 512 if cols % 512 == 0 else 256 if cols % 256 == 0 else 128
    tiles = cols // tile

    def hop(c, j):
        at = pl.ds(j * tile, tile)
        return pltpu.make_async_remote_copy(
            src_ref=out.at[c, :, at],
            dst_ref=whole.at[c, core, :, at],
            send_sem=hop_send.at[c, j],
            recv_sem=hop_recv.at[c, j],
            device_id={pipe: pos + 1},
            device_id_type=MESH,
        )

    def sibling(c, j):
        at = pl.ds(j * tile, tile)
        return pltpu.make_async_remote_copy(
            src_ref=whole.at[c, core, :, at],
            dst_ref=whole.at[c, core, :, at],
            send_sem=sib_send.at[c, j],
            recv_sem=sib_recv.at[c, j],
            device_id={"mp": 1 - core},
            device_id_type=MESH,
        )

    def part(c):
        return pltpu.make_async_remote_copy(
            src_ref=part_out.at[c],
            dst_ref=part_in.at[c],
            send_sem=part_send.at[c],
            recv_sem=part_recv.at[c],
            device_id={"mp": 1 - core},
            device_id_type=MESH,
        )

    def back(c):
        return pltpu.make_async_remote_copy(
            src_ref=cot_out.at[c],
            dst_ref=cot_in.at[c],
            send_sem=back_send.at[c],
            recv_sem=back_recv.at[c],
            device_id={pipe: pos - 1},
            device_id_type=MESH,
        )

    def probe_at(half, k, at):
        start = half * cols + at.start
        if not isinstance(start, int):
            start = pl.multiple_of(start, 128)
        return probe_all[k : k + 1, pl.ds(start, tile)]

    def rows(k):
        return pl.ds(k * tokens, tokens)

    acc_ref[...] = jnp.zeros_like(acc_ref)

    if crossed:
        drain_gather = crossed_gather(
            inputs_arg, target_arg, gain_arg, probe_block_ref, weight_block_ref, weight_all, probe_all, *crossed_scratch
        )
    else:
        drain_gather = straight_gather(
            pos, last, core, weight_block_ref, weight_all, probe_block_ref, probe_all,
            right_send, right_recv, left_send, left_recv, probe_send, probe_recv, own_sem,
        )

    def forward(c):
        @pl.when(pos == 0)
        def _():
            for half in range(2):
                whole[c, half, 0:tokens, :] = inputs_ref[c, :, half * cols : (half + 1) * cols]
                whole[c, half, tokens:, :] = jnp.zeros((dirs * tokens, cols), BF16)

        @pl.when(pos > 0)
        def _():
            for j in range(tiles):
                hop(c, j).wait_recv()
                sibling(c, j).start()
            for j in range(tiles):
                sibling(c, j).wait_recv()

        square = jnp.zeros((tokens, 128), F32)
        cross = [jnp.zeros((tokens, 128), F32) for _ in range(dirs)]
        for half in range(2):
            for j in range(tiles):
                at = pl.ds(j * tile, tile)
                h = whole[c, half, rows(0), at].astype(F32)
                square = square + fold(h * h)
                for k in range(dirs):
                    cross[k] = cross[k] + fold(h * whole[c, half, rows(k + 1), at].astype(F32))
        s = lax.rsqrt(jnp.sum(square, axis=-1, keepdims=True) / features + EPS)
        cube = -(s * s * s) / features
        u = [cube * jnp.sum(cross[k], axis=-1, keepdims=True) for k in range(dirs)]
        stats[c, 0] = jnp.broadcast_to(s, (tokens, 128))
        for k in range(dirs):
            stats[c, k + 1] = jnp.broadcast_to(u[k], (tokens, 128))
        for half in range(2):
            for j in range(tiles):
                at = pl.ds(j * tile, tile)
                h = whole[c, half, rows(0), at].astype(F32)
                gain = gain_ref[half, :, at]
                n = h * s
                operand[half, rows(0), at] = (n * gain).astype(BF16)
                for k in range(dirs):
                    t = whole[c, half, rows(k + 1), at].astype(F32)
                    mixed = (t * s + h * u[k]) * gain + n * probe_at(half, k, at)
                    operand[half, rows(k + 1), at] = mixed.astype(BF16)

        for j in range(tiles):
            at = pl.ds(j * tile, tile)
            a = jnp.dot(operand[0], weight_all[0:cols, at], preferred_element_type=F32)
            a = a + jnp.dot(operand[1], weight_all[cols:, at], preferred_element_type=F32)
            b = jnp.tanh(a[0:tokens])
            slope = 1.0 - b * b
            act[c, rows(0), at] = b
            out[c, rows(0), at] = (whole[c, core, rows(0), at].astype(F32) + b).astype(BF16)
            for k in range(1, dirs + 1):
                bk = slope * a[k * tokens : (k + 1) * tokens]
                act[c, rows(k), at] = bk
                out[c, rows(k), at] = (whole[c, core, rows(k), at].astype(F32) + bk).astype(BF16)

            @pl.when(pos < last)
            def _(j=j):
                hop(c, j).start()

    def backward(c):
        @pl.when(pos == last)
        def _():
            error = out[c, rows(0), :].astype(F32) - target_ref[c].astype(F32)
            cot_in[c, rows(0), :] = error.astype(BF16)
            cot_in[c, tokens:, :] = out[c, tokens:, :]

        @pl.when(pos < last)
        def _():
            back(c).wait_recv()

        for j in range(tiles):
            at = pl.ds(j * tile, tile)
            c0 = cot_in[c, rows(0), at].astype(F32)
            b = act[c, rows(0), at]
            slope = 1.0 - b * b
            twice = 2.0 * b * c0
            gstack[rows(0), at] = (c0 * slope).astype(BF16)
            for k in range(1, dirs + 1):
                ck = cot_in[c, rows(k), at].astype(F32)
                gstack[rows(k), at] = (ck * slope - twice * act[c, rows(k), at]).astype(BF16)

        s = stats[c, 0, :, 0:1]
        u = [stats[c, k + 1, :, 0:1] for k in range(dirs)]

        def product(j, sums):
            half = j // tiles
            at = pl.ds((j % tiles) * tile, tile)
            q_all = lax.dot_general(
                gstack[...],
                weight_all[pl.ds(j * tile, tile), :],
                (((1,), (1,)), ((), ())),
                preferred_element_type=F32,
            )
            q[half, :, at] = q_all
            h = whole[c, half, rows(0), at].astype(F32)
            gain = gain_ref[half, :, at]
            q0 = q_all[0:tokens]
            n = h * s
            p = q0 * gain
            new = [sums[0] + fold(p * h)]
            for k in range(dirs):
                t = whole[c, half, rows(k + 1), at].astype(F32)
                qk = q_all[(k + 1) * tokens : (k + 2) * tokens]
                v = t * s + h * u[k]
                pk = qk * gain + q0 * probe_at(half, k, at)
                new.append(sums[k + 1] + fold(pk * h + p * t))
                acc_ref[half, k : k + 1, at] += jnp.sum(qk * n + q0 * v, axis=0, keepdims=True)
            return tuple(new)

        zero = jnp.zeros((tokens, 128), F32)
        sums = (zero,) * (dirs + 1)
        for j in range(2 * tiles):
            sums = product(j, sums)

        @pl.when(pos > 0)
        def _():
            w = [jnp.sum(value, axis=-1, keepdims=True) for value in sums]
            cube = s * s * s / features
            w0 = cube * w[0]
            pull = [(3.0 / features) * s * s * u[k] * w[0] + cube * w[k + 1] for k in range(dirs)]

            def leaving(half, at):
                h = whole[c, half, rows(0), at].astype(F32)
                gain = gain_ref[half, :, at]
                q0 = q[half, rows(0), at]
                p = q0 * gain
                yield s * p - h * w0
                for k in range(dirs):
                    t = whole[c, half, rows(k + 1), at].astype(F32)
                    pk = q[half, rows(k + 1), at] * gain + q0 * probe_at(half, k, at)
                    yield u[k] * p + s * pk - h * pull[k] - t * w0

            for j in range(tiles):
                at = pl.ds(j * tile, tile)
                for k, value in enumerate(leaving(1 - core, at)):
                    part_out[c, rows(k), at] = value.astype(BF16)
            exchange = part(c)
            exchange.start()
            for j in range(tiles):
                at = pl.ds(j * tile, tile)
                for k, value in enumerate(list(leaving(core, at))):
                    q[core, rows(k), at] = value + cot_in[c, rows(k), at].astype(F32)
            exchange.wait_recv()
            for j in range(tiles):
                at = pl.ds(j * tile, tile)
                cot_out[c, :, at] = (q[core, :, at] + part_in[c, :, at].astype(F32)).astype(BF16)
            back(c).start()

    lag = jnp.minimum(lag_step * (last - pos), chunks)

    def turn(i, carry):
        @pl.when(i < chunks)
        def _():
            forward(jnp.minimum(i, chunks - 1))

        @pl.when((i >= lag) & (i - lag < chunks))
        def _():
            backward(jnp.clip(i - lag, 0, chunks - 1))

        return carry

    lax.fori_loop(0, chunks + min(lag_step * last, chunks), turn, 0)

    def drain(c, carry):
        @pl.when(pos < last)
        def _():
            for j in range(tiles):
                hop(c, j).wait_send()

        @pl.when(pos > 0)
        def _():
            for j in range(tiles):
                sibling(c, j).wait_send()
            part(c).wait_send()
            back(c).wait_send()

        return carry

    lax.fori_loop(0, chunks, drain, 0)

    drain_gather()


def settle_kernel(scale, divisor, crossed, parts_ref, probe_ref, hvp_ref, next_ref, got, tiles, sends, recvs, tile_sends, tile_recvs):
    owners, dirs, width = parts_ref.shape
    sections = lax.axis_size("section")
    dp, pos, core = lax.axis_index("dp"), lax.axis_index("section"), lax.axis_index("mp")
    pairs = [(i, j) for i in range(dirs) for j in range(i + 1)]
    group = 2 * owners
    everyone = owners * sections
    me = dp * 2 + core
    place = dp * sections + pos

    barrier = pltpu.get_barrier_semaphore()

    def greet_owner(step, carry):
        peer = lax.rem(me + step, group)
        target = {"dp": peer // 2, "mp": lax.rem(peer, 2)}
        pl.semaphore_signal(barrier, inc=1, device_id=target, device_id_type=MESH)
        return carry

    def greet_other(step, carry):
        target = {"dp": lax.rem(step, owners), "section": lax.rem(pos + 1 + step // owners, sections)}
        pl.semaphore_signal(barrier, inc=1, device_id=target, device_id_type=MESH)
        return carry

    def greet_all(step, carry):
        peer = lax.rem(place * 2 + core + step, 2 * everyone)
        spot = peer // 2
        target = {"dp": spot // sections, "section": lax.rem(spot, sections), "mp": lax.rem(peer, 2)}
        pl.semaphore_signal(barrier, inc=1, device_id=target, device_id_type=MESH)
        return carry

    if crossed:
        lax.fori_loop(1, 2 * everyone, greet_all, 0)
        pl.semaphore_wait(barrier, 2 * everyone - 1)
    else:
        lax.fori_loop(1, group, greet_owner, 0)
        lax.fori_loop(0, owners * (sections - 1), greet_other, 0)
        pl.semaphore_wait(barrier, group - 1 + owners * (sections - 1))

    def give(step):
        peer = lax.rem(me + step, group)
        return pltpu.make_async_remote_copy(
            src_ref=parts_ref.at[peer // 2],
            dst_ref=got.at[step],
            send_sem=sends.at[step],
            recv_sem=recvs.at[step],
            device_id={"dp": peer // 2, "mp": lax.rem(peer, 2)},
            device_id_type=MESH,
        )

    def start_give(step, carry):
        give(step).start()
        return carry

    def take(step, total):
        give(step).wait_recv()
        return total + got[step]

    def cross(slot):
        spot = pos * 2 + core
        return pltpu.make_async_remote_copy(
            src_ref=parts_ref.at[slot // 2],
            dst_ref=got.at[spot],
            send_sem=sends.at[slot],
            recv_sem=recvs.at[spot],
            device_id={"dp": slot // 2, "section": dp, "mp": lax.rem(slot, 2)},
            device_id_type=MESH,
        )

    def cross_in(slot):
        return pltpu.make_async_remote_copy(
            src_ref=got.at[slot],
            dst_ref=got.at[slot],
            send_sem=sends.at[slot],
            recv_sem=recvs.at[slot],
            device_id={"dp": pos, "section": slot // 2, "mp": lax.rem(slot, 2)},
            device_id_type=MESH,
        )

    def away(slot):
        return ~((dp == pos) & (slot == pos * 2 + core))

    if crossed:
        for slot in range(group):

            @pl.when(away(slot))
            def _():
                cross(slot).start()

        @pl.when(dp == pos)
        def _():
            got[pos * 2 + core] = parts_ref[dp]

        total = jnp.zeros(probe_ref.shape, F32)
        for slot in range(group):

            @pl.when(away(slot))
            def _():
                cross_in(slot).wait_recv()

            total = total + got[slot]
        curvature = total / divisor
    else:
        lax.fori_loop(1, group, start_give, 0)
        curvature = lax.fori_loop(1, group, take, parts_ref[dp]) / divisor
    hvp_ref[...] = curvature
    moved = probe_ref[...] + ETA * curvature
    row = lax.broadcasted_iota(jnp.int32, (16, 128), 0)
    tile = jnp.zeros((16, 128), F32)
    for index, (i, j) in enumerate(pairs):
        inner = jnp.sum(moved[i : i + 1] * moved[j : j + 1], axis=1, keepdims=True)
        tile = jnp.where(row == index, inner, tile)
    tiles[0] = tile

    def tell(step):
        peer = lax.rem(place + step, everyone)
        return pltpu.make_async_remote_copy(
            src_ref=tiles.at[0],
            dst_ref=tiles.at[step],
            send_sem=tile_sends.at[step],
            recv_sem=tile_recvs.at[step],
            device_id={"dp": peer // sections, "section": lax.rem(peer, sections)},
            device_id_type=MESH,
        )

    def start_tell(step, carry):
        tell(step).start()
        return carry

    lax.fori_loop(1, everyone, start_tell, 0)

    def hear(step, carry):
        tell(step).wait_recv()
        return carry

    lax.fori_loop(1, everyone, hear, 0)
    gram = lax.fori_loop(
        0,
        everyone,
        lambda source, total: total + tiles[lax.rem(place - source + everyone, everyone)],
        jnp.zeros((16, 128), F32),
    )
    entry = {pair: gram[index : index + 1, 0:1] for index, pair in enumerate(pairs)}
    factor = {}
    for j in range(dirs):
        rest = entry[j, j]
        for k in range(j):
            rest = rest - factor[j, k] * factor[j, k]
        factor[j, j] = jnp.sqrt(rest)
        for i in range(j + 1, dirs):
            rest = entry[i, j]
            for k in range(j):
                rest = rest - factor[i, k] * factor[j, k]
            factor[i, j] = rest / factor[j, j]
    solved = []
    for i in range(dirs):
        value = moved[i : i + 1]
        for k in range(i):
            value = value - factor[i, k] * solved[k]
        solved.append(value / factor[i, i])
        next_ref[i : i + 1, :] = solved[i] * scale

    def drain_give(step, carry):
        give(step).wait_send()
        return carry

    def drain_tell(step, carry):
        tell(step).wait_send()
        return carry

    if crossed:
        for slot in range(group):

            @pl.when(away(slot))
            def _():
                cross(slot).wait_send()

    else:
        lax.fori_loop(1, group, drain_give, 0)
    lax.fori_loop(1, everyone, drain_tell, 0)


def settle(accumulated, own_probe, scale, divisor, crossed):
    dirs, width = own_probe.shape
    owners, sections = lax.axis_size("dp"), lax.axis_size("section")
    vmem = pl.BlockSpec(memory_space=pltpu.VMEM)
    return pl.pallas_call(
        functools.partial(settle_kernel, scale, divisor, crossed),
        out_shape=[jax.ShapeDtypeStruct((dirs, width), F32)] * 2,
        in_specs=[vmem] * 2,
        out_specs=[vmem] * 2,
        scratch_shapes=[
            pltpu.VMEM((2 * owners, dirs, width), F32),
            pltpu.VMEM((owners * sections, 16, 128), F32),
        ]
        + [pltpu.SemaphoreType.DMA((2 * owners,))] * 2
        + [pltpu.SemaphoreType.DMA((owners * sections,))] * 2,
        compiler_params=pltpu.CompilerParams(
            collective_id=1, has_side_effects=True, vmem_limit_bytes=16 * 1024 * 1024
        ),
    )(accumulated.reshape(dirs, owners, width).transpose(1, 0, 2), own_probe)


def relay(inputs, target, gain, probe, weight, sections, chunk_tokens, lag_step, crossed):
    features = inputs.shape[-1]
    cols = features // 2
    dirs = probe.shape[0]
    chunks = inputs.shape[0] * inputs.shape[1] // chunk_tokens
    height = (dirs + 1) * chunk_tokens
    vmem = pl.BlockSpec(memory_space=pltpu.VMEM)
    dma = pltpu.SemaphoreType.DMA((chunks,))
    ring = pltpu.SemaphoreType.DMA((lax.axis_size("dp"),))
    extra = []
    if crossed:
        extra = [
            pltpu.VMEM((chunks, chunk_tokens, features), BF16),
            pltpu.VMEM((chunks, chunk_tokens, cols), BF16),
            pltpu.VMEM((2, 1, cols), F32),
            pltpu.VMEM((sections, weight.shape[0] // sections, cols), BF16),
            pltpu.SemaphoreType.DMA((15, sections)),
            pltpu.SemaphoreType.DMA((2,)),
            pltpu.SemaphoreType.DMA((5,)),
        ]
    acc = pl.pallas_call(
        functools.partial(relay_kernel, sections, lag_step, crossed),
        out_shape=jax.ShapeDtypeStruct((2, dirs, cols), F32),
        in_specs=[vmem] * 4 + [pl.BlockSpec(memory_space=pl.ANY)],
        out_specs=vmem,
        scratch_shapes=[
            pltpu.VMEM((features, cols), BF16),
            pltpu.VMEM((dirs, features), F32),
            pltpu.VMEM((chunks, 2, height, cols), BF16),
            pltpu.VMEM((chunks, height, cols), F32),
            pltpu.VMEM((chunks, height, cols), BF16),
            pltpu.VMEM((chunks, height, cols), BF16),
            pltpu.VMEM((chunks, height, cols), BF16),
            pltpu.VMEM((chunks, height, cols), BF16),
            pltpu.VMEM((chunks, height, cols), BF16),
            pltpu.VMEM((2, height, cols), BF16),
            pltpu.VMEM((height, cols), BF16),
            pltpu.VMEM((2, height, cols), F32),
            pltpu.VMEM((chunks, dirs + 1, chunk_tokens, 128), F32),
        ]
        + [pltpu.SemaphoreType.DMA((chunks, cols // 128))] * 4
        + [dma] * 4
        + [ring] * 6
        + [pltpu.SemaphoreType.DMA]
        + extra,
        compiler_params=pltpu.CompilerParams(
            collective_id=0, has_side_effects=True, vmem_limit_bytes=56 * 1024 * 1024
        ),
        cost_estimate=pl.CostEstimate(
            flops=4 * chunks * height * features * cols, bytes_accessed=2 * features * cols, transcendentals=0
        ),
    )(
        inputs.reshape(chunks, chunk_tokens, features),
        target.reshape(chunks, chunk_tokens, cols),
        gain.reshape(2, 1, cols),
        probe,
        weight,
    )
    return acc.transpose(1, 0, 2).reshape(dirs, features)


def local(inputs, target, gains, weights, probes):
    sections = lax.axis_size("section")
    batches, micro_batch_tokens, features = inputs.shape
    probe_block = probes[:, 0, :]
    crossed = lax.axis_size("dp") == sections == 4 and probe_block.shape[1] % 128 == 0 and weights.shape[1] % 128 == 0
    if probe_block.shape[1] % 128:
        probe_block = lax.all_gather(probe_block, "dp", axis=1, tiled=True)
    accumulated = relay(inputs, target, gains[0], probe_block, weights[0], sections, 16, 3, crossed)
    divisor = batches * micro_batch_tokens * lax.axis_size("dp")
    curvature, rotated = settle(accumulated, probes[:, 0, :], math.sqrt(sections * features), divisor, crossed)
    return (curvature[:, None, :], rotated[:, None, :])


def solution(mesh):
    in_specs = (
        P(None, "dp", None),
        P(None, "dp", "mp"),
        P("section", None),
        P("section", "dp", "mp"),
        P(None, "section", "dp"),
    )
    out_specs = (P(None, "section", "dp"), P(None, "section", "dp"))
    return jax.shard_map(local, mesh=mesh, in_specs=in_specs, out_specs=out_specs, check_vma=False)
```
